32 devices in a mesh: shot: 2 (over y), gx: 4 (over z), gy: 2 (over x), gz: 2 (over core).
Axes of the slice: x: 2, y: 2, z: 4, core: 2. Of those that a mesh axis runs over, the one named last changes fastest.
Arguments:
- source_prev: float32 [96, 8, 1024], P(('shot', 'gx'), 'gy', 'gz'), parts along dimension 0, may hold values from -6 to 6
- source_now: float32 [96, 8, 1024], P(('shot', 'gx'), 'gy', 'gz'), parts along dimension 0, may hold values from -6 to 6
- receiver_prev: float32 [96, 8, 1024], P(('shot', 'gx'), 'gy', 'gz'), parts along dimension 0, may hold values from -6 to 6
- receiver_now: float32 [96, 8, 1024], P(('shot', 'gx'), 'gy', 'gz'), parts along dimension 0, may hold values from -6 to 6
- courant: float32 [48, 8, 1024], P('gx', 'gy', 'gz'), may hold values from 0.04 to 0.16
- absorbing: int32 [48, 8, 1024], P('gx', 'gy', 'gz'), may hold values from 0 to 8, as said below
- source_cell: int32 [6], P('shot'), parts along dimension 0, may hold values from 0 to 1023, as said below
- wavelet: float32 [8], P('shot'), parts along dimension 0, may hold values from -4 to 4
- receiver_cells: int32 [256, 2], P('shot'), parts along dimension 0, may hold values from 0 to 47, as said below
- traces: float32 [4, 256], P(None, 'shot'), parts along dimension 1, may hold values from -6 to 6
Outputs:
- source_field: float32 [96, 8, 1024], P(('shot', 'gx'), 'gy', 'gz'), parts along dimension 0
- receiver_field: float32 [96, 8, 1024], P(('shot', 'gx'), 'gy', 'gz'), parts along dimension 0
- filtered_image: bfloat16 [16, 96, 8, 1024], P(None, ('shot', 'gx'), 'gy', 'gz'), parts along dimension 1
The draws below stay inside these ranges and needn't reach their ends.
There are 2 independent parts, one for each index of `shot`. The reference program is written for one: setup_inputs(seed, part) draws one part's arguments, and reference() takes and returns one part's arrays. A program takes and returns all parts, laid end to end along the dimension named above; an argument that names none is the same for every part. Nothing has to cross between parts.
Inputs may be any that keep to these rules, and one draw needn't show every extreme that they name: `source_cell`: the source's cell as (x, y, z), each coordinate within the grid. `receiver_cells`: each row is a receiver's (x, y) within the grid, on the top surface at depth 0; several receivers may share a cell. Depth of a cell into the absorbing layers along the four side faces and the bottom face, largest at the grid's faces; 0 in the interior; the top face has no layer.
All inputs are finite; a program needn't handle non-finite values.
Results may differ from the reference program's by a relative error of at most 0.001.
Values sent between devices are 32-bit elements; how exact they have to be, the bound alone decides.
A program may use at most 64 MiB of HBM per device.

```python
import math
import jax
import jax.numpy as jnp
from jax import lax

LAGS = 16
STEPS = 4
EVERY = 2
NX = 48
NY = 8
NZ = 1024
NREC = 128


def draw_absorbing(key, part):
    sides = jax.random.randint(jax.random.fold_in(key, 11), (4,), 2, 9)
    x_cells = jnp.arange(NX, dtype=jnp.int32)
    y_cells = jnp.arange(NY, dtype=jnp.int32)
    z_cells = jnp.arange(NZ, dtype=jnp.int32)
    level_x = jnp.maximum(jnp.maximum(sides[0] - x_cells, sides[1] - (NX - 1 - x_cells)), 0)
    level_y = jnp.maximum(jnp.maximum(sides[2] - y_cells, sides[3] - (NY - 1 - y_cells)), 0)
    level_z = jnp.maximum(8 - (NZ - 1 - z_cells), 0)
    level = jnp.maximum(jnp.maximum(level_x[:, None, None], level_y[None, :, None]), level_z[None, None, :])
    return level.astype(jnp.int32)


def draw_source_cell(key, part):
    first = jax.random.randint(jax.random.fold_in(key, 21), (), 0, NX)
    second = jax.random.randint(jax.random.fold_in(key, 22), (), 0, NY)
    third = jax.random.randint(jax.random.fold_in(key, 23), (), 0, NZ)
    return jnp.stack([first, second, third]).astype(jnp.int32)


def draw_receiver_cells(key, part):
    first = jax.random.randint(jax.random.fold_in(key, 31), (NREC,), 0, NX)
    second = jax.random.randint(jax.random.fold_in(key, 32), (NREC,), 0, NY)
    return jnp.stack([first, second], axis=1).astype(jnp.int32)


def levels(key, shape, cuts, low, high):
    loudness, own = 1.0, jax.random.fold_in(key, 6)
    for dim, blocks in cuts:
        heights = jnp.exp(jax.random.uniform(jax.random.fold_in(own, dim), (blocks,), jnp.float32, low / len(cuts), high / len(cuts)))
        loudness = loudness * jnp.repeat(heights, shape[dim] // blocks).reshape([-1 if axis == dim else 1 for axis in range(len(shape))])
    return loudness


def bell_draw(rng, shape, spread, limit, split=(), kind=jnp.bfloat16):
    result = spread * jax.random.normal(rng, shape, jnp.float32)
    if split:
        result = result * levels(rng, shape, split, -0.22, 0.18)
    return jnp.clip(result, -limit, limit).astype(kind)


def setup_inputs(seed: int = 0, part: int = 0) -> dict:
    splits = jax.random.split(jax.random.key(seed), 11)
    part_keys = jax.random.split(jax.random.fold_in(splits[10], part), 11)
    return {
        "source_prev": bell_draw(part_keys[0], (NX, NY, NZ), 1.0, 6.0, ((0, 4), (1, 2), (2, 2)), jnp.float32),
        "source_now": bell_draw(part_keys[1], (NX, NY, NZ), 1.0, 6.0, ((0, 4), (1, 2), (2, 2)), jnp.float32),
        "receiver_prev": bell_draw(part_keys[2], (NX, NY, NZ), 1.0, 6.0, ((0, 4), (1, 2), (2, 2)), jnp.float32),
        "receiver_now": bell_draw(part_keys[3], (NX, NY, NZ), 1.0, 6.0, ((0, 4), (1, 2), (2, 2)), jnp.float32),
        "courant": jnp.clip(jnp.exp(math.log(0.16) - 1.3862944 * jax.random.uniform(splits[4], (NX, NY, NZ), jnp.float32) ** levels(splits[4], (NX, NY, NZ), ((0, 4), (1, 2), (2, 2)), -0.2, 0.2)), 0.04, 0.16),
        "absorbing": draw_absorbing(jax.random.fold_in(splits[10], 71), part),
        "source_cell": draw_source_cell(jax.random.fold_in(jax.random.fold_in(splits[10], part), 71), part),
        "wavelet": bell_draw(part_keys[7], (STEPS,), 1.0, 4.0, (), jnp.float32),
        "receiver_cells": draw_receiver_cells(jax.random.fold_in(jax.random.fold_in(splits[10], part), 71), part),
        "traces": bell_draw(part_keys[9], (STEPS, NREC), 1.0, 6.0, (), jnp.float32),
    }


stencil_weights = (8.0 / 5.0, -1.0 / 5.0, 8.0 / 315.0, -1.0 / 560.0)
centre_weight = -205.0 / 72.0


def stencil(padded):
    size_x = padded.shape[-3] - 8
    size_y = padded.shape[-2] - 8
    size_z = padded.shape[-1] - 8

    def window(start_x, start_y, start_z):
        return padded[..., start_x:start_x + size_x, start_y:start_y + size_y, start_z:start_z + size_z]

    total = (3.0 * centre_weight) * window(4, 4, 4)
    for reach, weight in enumerate(stencil_weights, 1):
        total = total + weight * (window(4 + reach, 4, 4) + window(4 - reach, 4, 4) + window(4, 4 + reach, 4) + window(4, 4 - reach, 4) + window(4, 4, 4 + reach) + window(4, 4, 4 - reach))
    return total


def advance(padded, current, earlier, courant, damping):
    return (2.0 * current - (1.0 - damping) * earlier + courant * stencil(padded)) / (1.0 + damping)


def laplace(padded):
    size_x = padded.shape[-3] - 2
    size_y = padded.shape[-2] - 2
    size_z = padded.shape[-1] - 2

    def window(start_x, start_y, start_z):
        return padded[..., start_x:start_x + size_x, start_y:start_y + size_y, start_z:start_z + size_z]

    return 6.0 * window(1, 1, 1) - (window(2, 1, 1) + window(0, 1, 1) + window(1, 2, 1) + window(1, 0, 1) + window(1, 1, 2) + window(1, 1, 0))


def reference(source_prev, source_now, receiver_prev, receiver_now, courant, absorbing, source_cell, wavelet, receiver_cells, traces):
    earlier = jnp.stack([source_prev, receiver_prev])
    current = jnp.stack([source_now, receiver_now])
    damping = absorbing.astype(jnp.float32) / 16.0
    snapshots = []
    for step_index in range(STEPS):
        padded = jnp.pad(current, ((0, 0), (4, 4), (4, 4), (4, 4)))
        upcoming = advance(padded, current, earlier, courant, damping)
        upcoming = upcoming.at[0, source_cell[0], source_cell[1], source_cell[2]].add(wavelet[step_index])
        upcoming = upcoming.at[1, receiver_cells[:, 0], receiver_cells[:, 1], 0].add(traces[step_index])
        earlier, current = current, upcoming
        if (step_index + 1) % EVERY == 0:
            snapshots.append(jnp.pad(current, ((0, 0), (LAGS // 2, LAGS // 2), (0, 0), (0, 0))))

    def one_lag(offset):
        image = jnp.zeros((NX, NY, NZ), jnp.float32)
        for widened in snapshots:
            image = image + lax.dynamic_slice_in_dim(widened[0], (LAGS - offset).astype(jnp.int32), NX, 0) * lax.dynamic_slice_in_dim(widened[1], offset.astype(jnp.int32), NX, 0)
        return laplace(jnp.pad(image, 1)).astype(jnp.bfloat16)

    filtered_image = lax.map(one_lag, jnp.arange(LAGS, dtype=jnp.int32))
    return current[0], current[1], filtered_image
```

```python
import functools
import jax
import jax.numpy as jnp
from jax import lax
from jax.experimental import pallas as pl
from jax.experimental.pallas import tpu as pltpu
from jax.sharding import PartitionSpec as P

LAGS = 16
STEPS = 4
EVERY = 2
HALF = LAGS // 2
H = HALF + 1
REACH = 4
LANES = 128

W1, W2, W3, W4 = (8.0 / 5.0, -1.0 / 5.0, 8.0 / 315.0, -1.0 / 560.0)
centre_weight = -205.0 / 72.0
MESH = pl.DeviceIdType.MESH


def kernel(
    sp, sn, rp, rn, cr, ab, cell, wav, rc, tr,
    out_s, out_r, out_i,
    F, YB, YC, ZL, ZR, PS, YPB, YPC, E, G, GE, D, DG, CA, CB, CC, INJ, IM, IH, LP, ST,
    send, recv,
):
    tx, ty, tz = sn.shape
    nchunk = tx // REACH
    nx, ny, nz = (lax.axis_size(a) for a in ("gx", "gy", "gz"))
    ix, iy, iz = (lax.axis_index(a) for a in ("gx", "gy", "gz"))
    copies = []

    def exists(dx, dy, dz):
        ok = None
        for d, i, n in ((dx, ix, nx), (dy, iy, ny), (dz, iz, nz)):
            if d:
                here = (i + d >= 0) & (i + d < n)
                ok = here if ok is None else ok & here
        return ok

    def device(dx, dy, dz):
        return {
            a: i + d for a, i, d in (("gx", ix, dx), ("gy", iy, dy), ("gz", iz, dz)) if d
        }

    class Copy:
        def __init__(self, src, dst, direction):
            number = len(copies)
            self.desc = pltpu.make_async_remote_copy(
                src_ref=src,
                dst_ref=dst,
                send_sem=send.at[number],
                recv_sem=recv.at[number],
                device_id=device(*direction),
                device_id_type=MESH,
            )
            self.out = exists(*direction)
            self.into = exists(*(-d for d in direction))
            copies.append(self)
            pl.when(self.out)(lambda: self.desc.start())

        def wait(self):
            pl.when(self.into)(lambda: self.desc.wait_recv())

        def finish(self):
            pl.when(self.out)(lambda: self.desc.wait_send())

    lane = lax.broadcasted_iota(jnp.int32, (8, LANES), 1)
    sub_z = lax.broadcasted_iota(jnp.int32, (8, tz), 0)
    lane_z = lax.broadcasted_iota(jnp.int32, (8, tz), 1)
    even, odd = pl.ds(0, ty, 2), pl.ds(1, ty, 2)

    def each(low, high, body, unroll=1):
        def step(i, carry):
            body(i)
            return carry

        lax.fori_loop(low, high, step, 0, unroll=unroll)

    tiles = tz // LANES

    def weave(slot, x, a, b):
        for q in range(tiles):
            part = slice(q * LANES, (q + 1) * LANES)
            ST[slot, x, q, even, :] = a[:, part]
            ST[slot, x, q, odd, :] = b[:, part]
        return jnp.concatenate([ST[slot, x, q] for q in range(tiles)], axis=1)

    def unweave(x, v, at):
        for q in range(tiles):
            LP[x, q] = v[:, q * LANES : (q + 1) * LANES]
        return [
            jnp.concatenate([LP[x, q, rows, :] for q in range(tiles)], axis=1) for rows in at
        ]

    def load_now(x):
        F[1, H + x] = weave(0, x, sn[x], rn[x])

    each(0, tx, load_now)

    low_x, high_x = ix == 0, ix == nx - 1
    low_y, high_y = iy == 0, iy == ny - 1
    low_z, high_z = iz == 0, iz == nz - 1

    @pl.when(low_x)
    def _():
        for i in range(1, STEPS + 2):
            F[i, 0:H] = jnp.zeros((H, 8, tz), jnp.float32)

    @pl.when(high_x)
    def _():
        for i in range(1, STEPS + 2):
            F[i, H + tx : 2 * H + tx] = jnp.zeros((H, 8, tz), jnp.float32)

    for missing, buf, packed in ((low_y, YB, YPB), (high_y, YC, YPC)):

        @pl.when(missing)
        def _(buf=buf):
            buf[...] = jnp.zeros(buf.shape, jnp.float32)

        @pl.when(missing | low_x | high_x)
        def _(packed=packed):
            packed[...] = jnp.zeros(packed.shape, jnp.float32)

    for missing, buf in ((low_z, ZL), (high_z, ZR)):

        @pl.when(missing | low_x | high_x)
        def _(buf=buf):
            buf[...] = jnp.zeros(buf.shape, jnp.float32)

    signs = (-1, 1)
    around = [(s, 0, 0) for s in signs] + [(0, s, 0) for s in signs] + [(0, 0, s) for s in signs]
    around += [(s, r, 0) for s in signs for r in signs] + [(s, 0, r) for s in signs for r in signs]
    barrier = pltpu.get_barrier_semaphore()
    count = 0
    for direction in around:
        there = exists(*direction)
        count = count + there.astype(jnp.int32)

        @pl.when(there)
        def _(direction=direction):
            pl.semaphore_signal(
                barrier, inc=1, device_id=device(*direction), device_id_type=MESH
            )

    pl.semaphore_wait(barrier, count)

    def send_x(f, low, high):
        left = Copy(
            F.at[f, H + low : H + high],
            F.at[f, H + tx + low : H + tx + high],
            (-1, 0, 0),
        )
        right = Copy(
            F.at[f, H + tx - high : H + tx - low],
            F.at[f, H - high : H - low],
            (1, 0, 0),
        )
        return left, right

    def send_y(f, c):
        own = F.at[f, H + c * REACH : H + (c + 1) * REACH]
        there = pl.ds(c * REACH, REACH)
        return (
            Copy(own, YB.at[f - 1, there], (0, 1, 0)),
            Copy(own, YC.at[f - 1, there], (0, -1, 0)),
        )

    def send_z(f, low, high, dx=0):
        rows = pl.ds(H + low, high - low)
        there = pl.ds(H + low - dx * tx, high - low)
        return (
            Copy(F.at[f, rows, :, pl.ds(tz - LANES, LANES)], ZL.at[f - 1, there], (dx, 0, 1)),
            Copy(F.at[f, rows, :, pl.ds(0, LANES)], ZR.at[f - 1, there], (dx, 0, -1)),
        )

    def send_rows(f, s):
        def pack(g):
            first, last = F[f, H + g * REACH], F[f, H + g * REACH]
            last = pltpu.roll(last, 2, 0)
            for j in range(1, REACH):
                row = F[f, H + g * REACH + j]
                here = sub_z // 2 == j
                first = jnp.where(here, pltpu.roll(row, 2 * j, 0), first)
                shift = (2 * j - 6) % 8
                last = jnp.where(here, pltpu.roll(row, shift, 0) if shift else row, last)
            PS[s, 0, g] = first
            PS[s, 1, g] = last

        each(0, nchunk, pack)
        groups = HALF // REACH
        done = []
        for dy, side, buf in ((1, 1, YPB), (-1, 0, YPC)):
            done.append(
                Copy(PS.at[s, side], buf.at[s, groups : groups + nchunk], (0, dy, 0))
            )
            done.append(
                Copy(
                    PS.at[s, side, 0:groups],
                    buf.at[s, groups + nchunk : 2 * groups + nchunk],
                    (-1, dy, 0),
                )
            )
            done.append(
                Copy(
                    PS.at[s, side, nchunk - groups : nchunk],
                    buf.at[s, 0:groups],
                    (1, dy, 0),
                )
            )
        return done

    order = [0] + [nchunk - 1] * (nchunk > 1) + list(range(1, nchunk - 1))
    xw, yw, zw = {}, {}, {}
    xw[1] = send_x(1, 0, REACH)
    for c in order:
        yw[1, c] = send_y(1, c)
        zw[1, c] = send_z(1, c * REACH, (c + 1) * REACH)

    x_start, y_start, z_start = ix * tx, iy * ty, iz * tz

    def load_rest(x):
        F[0, H + x] = weave(1, x, sp[x], rp[x])
        damping = ab[x].astype(jnp.float32) / 16.0
        inverse = 1.0 / (1.0 + damping)
        c2 = cr[x] * inverse
        a2 = 2.0 * inverse + (3.0 * centre_weight) * c2
        b2 = (damping - 1.0) * inverse
        CA[x] = weave(2, x, a2, a2)
        CB[x] = weave(3, x, b2, b2)
        CC[x] = weave(4, x, c2, c2)
        rows = x * 8 + lax.broadcasted_iota(jnp.int32, (8, rc.shape[1]), 0)
        y_of = rc[1:2, :] - y_start
        where = (rc[0:1, :] - x_start) * 8 + y_of * 2 + 1
        where = jnp.where((y_of >= 0) & (y_of < ty), where, -1)
        top = jnp.where(iz == 0, 1.0, 0.0)
        for t in range(STEPS):
            total = jnp.sum(
                jnp.where(rows == where, tr[t : t + 1, :], 0.0), axis=1, keepdims=True
            )
            INJ[t, x] = jnp.where(lane == 0, total * top, 0.0)

    each(0, tx, load_rest)
    point = jnp.where(
        (lane_z == cell[2] - z_start) & (sub_z == (cell[1] - y_start) * 2), 1.0, 0.0
    )
    source_x = cell[0] - x_start

    def merge(f, s, low, high):
        def body(x):
            E[s, x] = jnp.where(lane < LANES // 2, ZR[f - 1, x], ZL[f - 1, x])

        each(H + low, H + high, body)

    def advance(t, c):
        f = t + 1

        def body(j):
            x = c * REACH + j
            cur = F[f, H + x]
            below, above = YB[t, x], YC[t, x]
            edge = jnp.where(lane < LANES // 2, ZR[t, H + x], ZL[t, H + x])
            row = jnp.concatenate([cur, edge], axis=1)
            wide = tz + LANES
            total = None
            for k, w in ((1, W1), (2, W2), (3, W3), (4, W4)):
                part = F[f, H + x + k] + F[f, H + x - k]
                part = part + (pltpu.roll(row, k, 1) + pltpu.roll(row, wide - k, 1))[:, :tz]
                if k == 4:
                    part = part + (above + below)
                total = w * part if total is None else total + w * part

            def up(k):
                return jnp.where(sub_z < 2 * k, above, cur)

            def down(k):
                return jnp.where(sub_z >= 8 - 2 * k, below, cur)

            total = total + pltpu.roll(W1 * up(1) + W3 * down(3), 6, 0)
            total = total + pltpu.roll(W2 * (up(2) + down(2)), 4, 0)
            total = total + pltpu.roll(W3 * up(3) + W1 * down(1), 2, 0)
            new = CA[x] * cur + CB[x] * F[f - 1, H + x] + CC[x] * total
            new = new + point * (wav[t] * (source_x == x).astype(jnp.float32))
            F[f + 1, H + x] = new
            F[f + 1, H + x, :, 0:LANES] = new[:, 0:LANES] + INJ[t, x]

        each(0, REACH, body, unroll=2)

    late = {}
    snaps = [t + 2 for t in range(STEPS) if (t + 1) % EVERY == 0]
    for t in range(STEPS):
        f = t + 1
        nf = f + 1
        last = t == STEPS - 1
        for number, c in enumerate(order):
            if number == 0:
                xw[f][1].wait()
                if nchunk == 1:
                    xw[f][0].wait()
            if number == 1:
                xw[f][0].wait()
            for w in yw[f, c] + zw[f, c]:
                w.wait()
            advance(t, c)
            if not last:
                yw[nf, c] = send_y(nf, c)
                zw[nf, c] = send_z(nf, c * REACH, (c + 1) * REACH)
                if number == min(1, nchunk - 1):
                    xw[nf] = send_x(nf, 0, REACH)
        if nf in snaps:
            s = snaps.index(nf)
            late[s] = list(send_x(nf, 0 if last else REACH, H))
            if last:
                late[s] += send_z(nf, 0, tx)
            late[s] += send_rows(nf, s)
            late[s] += send_z(nf, 0, HALF, -1)
            late[s] += send_z(nf, tx - HALF, tx, 1)

    def out_fields(x):
        out_s[x], out_r[x] = unweave(x, F[STEPS + 1, H + x], (even, odd))

    each(0, tx, out_fields)

    def swap(v):
        parity = lax.broadcasted_iota(jnp.int32, v.shape, 0) % 2
        return jnp.where(parity == 0, pltpu.roll(v, 7, 0), pltpu.roll(v, 1, 0))

    for s, f in enumerate(snaps):
        for w in late[s]:
            w.wait()
        merge(f, s, -HALF, tx + HALF)

        def swapped(x, s=s, f=f):
            G[s, x] = swap(F[f, x])

        each(0, tx + 2 * H, swapped)

        def swapped_edge(x, s=s):
            GE[s, x] = swap(E[s, x])

        each(H - HALF, H + tx + HALF, swapped_edge)

        def unpack(g, s=s):
            above, below = YPC[s, g], YPB[s, g]
            for j in range(REACH):
                first = pltpu.roll(above, (8 - 2 * j) % 8, 0) if j else above
                shift = (6 - 2 * j) % 8
                other = pltpu.roll(below, shift, 0) if shift else below
                both = jnp.where(sub_z < 4, first, other)
                D[s, g * REACH + j] = both
                DG[s, g * REACH + j] = swap(both)

        each(0, (tx + 2 * HALF) // REACH, unpack)

    nsnap = len(snaps)

    def image(m, keep_even, keep_odd):
        def product(x):
            a, b = HALF + x - m, HALF + x + m
            total = F[snaps[0], a] * G[0, b]
            for s in range(1, nsnap):
                total = total + F[snaps[s], a] * G[s, b]
            IM[x, :, 0:tz] = total

        each(0, tx + 2, product, unroll=2)

        def halo(x):
            a, b = H + x - m, H + x + m
            total = E[0, a] * GE[0, b]
            for s in range(1, nsnap):
                total = total + E[s, a] * GE[s, b]
            IM[x + 1, :, tz : tz + LANES] = total
            a, b = HALF + x - m, HALF + x + m
            total = D[0, a] * DG[0, b]
            for s in range(1, nsnap):
                total = total + D[s, a] * DG[s, b]
            IH[x] = total

        each(0, tx, halo, unroll=2)

        def laplace(x):
            row = IM[x + 1]
            centre, side = row[:, :tz], IH[x]
            wide = tz + LANES
            near = (pltpu.roll(row, 1, 1) + pltpu.roll(row, wide - 1, 1))[:, :tz]
            near = near + (IM[x, :, 0:tz] + IM[x + 2, :, 0:tz])
            near = near + pltpu.roll(jnp.where(sub_z < 2, side, centre), 6, 0)
            near = near + pltpu.roll(jnp.where(sub_z >= 6, side, centre), 2, 0)
            plus, minus = unweave(x, 6.0 * centre - near, (even, odd))
            if keep_even:
                out_i[HALF + m, x] = plus.astype(jnp.bfloat16)
            if keep_odd:
                out_i[HALF - m, x] = minus.astype(jnp.bfloat16)

        each(0, tx, laplace, unroll=2)

    image(0, True, False)
    each(1, HALF, lambda m: image(m, True, True))
    image(HALF, False, True)
    for c in copies:
        c.finish()


def local(
    source_prev,
    source_now,
    receiver_prev,
    receiver_now,
    courant,
    absorbing,
    source_cell,
    wavelet,
    receiver_cells,
    traces,
):
    tx, ty, tz = courant.shape
    nsnap = STEPS // EVERY
    nchunk = tx // REACH
    groups = (tx + 2 * HALF) // REACH
    f32 = jnp.float32
    vmem = pl.BlockSpec(memory_space=pltpu.VMEM)
    smem = pl.BlockSpec(memory_space=pltpu.SMEM)
    number = STEPS * (2 + 4 * nchunk) + nsnap * 14
    V = pltpu.VMEM
    return pl.pallas_call(
        kernel,
        out_shape=(
            jax.ShapeDtypeStruct((tx, ty, tz), f32),
            jax.ShapeDtypeStruct((tx, ty, tz), f32),
            jax.ShapeDtypeStruct((LAGS, tx, ty, tz), jnp.bfloat16),
        ),
        in_specs=[vmem] * 6 + [smem] * 2 + [vmem] * 2,
        out_specs=(vmem, vmem, vmem),
        scratch_shapes=[
            V((STEPS + 2, tx + 2 * H, 8, tz), f32),
            V((STEPS, tx, 8, tz), f32),
            V((STEPS, tx, 8, tz), f32),
            V((STEPS + 1, tx + 2 * H, 8, LANES), f32),
            V((STEPS + 1, tx + 2 * H, 8, LANES), f32),
            V((nsnap, 2, nchunk, 8, tz), f32),
            V((nsnap, groups, 8, tz), f32),
            V((nsnap, groups, 8, tz), f32),
            V((nsnap, tx + 2 * H, 8, LANES), f32),
            V((nsnap, tx + 2 * H, 8, tz), f32),
            V((nsnap, tx + 2 * H, 8, LANES), f32),
            V((nsnap, tx + 2 * HALF, 8, tz), f32),
            V((nsnap, tx + 2 * HALF, 8, tz), f32),
            V((tx, 8, tz), f32),
            V((tx, 8, tz), f32),
            V((tx, 8, tz), f32),
            V((STEPS, tx, 8, LANES), f32),
            V((tx + 2, 8, tz + LANES), f32),
            V((tx, 8, tz), f32),
            V((tx, tz // LANES, 8, LANES), f32),
            V((5, tx, tz // LANES, 8, LANES), f32),
            pltpu.SemaphoreType.DMA((number,)),
            pltpu.SemaphoreType.DMA((number,)),
        ],
        compiler_params=pltpu.CompilerParams(
            collective_id=0, has_side_effects=True, vmem_limit_bytes=40 * 2**20
        ),
    )(
        source_prev,
        source_now,
        receiver_prev,
        receiver_now,
        courant,
        absorbing,
        source_cell,
        wavelet,
        receiver_cells.T,
        traces,
    )


def solution(mesh):
    placed = (
        P(("shot", "gx"), "gy", "gz"),
        P(("shot", "gx"), "gy", "gz"),
        P(("shot", "gx"), "gy", "gz"),
        P(("shot", "gx"), "gy", "gz"),
        P("gx", "gy", "gz"),
        P("gx", "gy", "gz"),
        P("shot"),
        P("shot"),
        P("shot", None),
        P(None, "shot"),
    )
    return jax.shard_map(
        local,
        mesh=mesh,
        in_specs=placed,
        out_specs=(
            P(("shot", "gx"), "gy", "gz"),
            P(("shot", "gx"), "gy", "gz"),
            P(None, ("shot", "gx"), "gy", "gz"),
        ),
        check_vma=False,
    )
```

```python
import functools
import jax
import jax.numpy as jnp
from jax import lax
from jax.experimental import pallas as pl
from jax.experimental.pallas import tpu as pltpu
from jax.sharding import PartitionSpec as P

LAGS = 16
STEPS = 4
EVERY = 2
HALF = LAGS // 2
H = HALF + 1
REACH = 4
LANES = 128

W1, W2, W3, W4 = (8.0 / 5.0, -1.0 / 5.0, 8.0 / 315.0, -1.0 / 560.0)
centre_weight = -205.0 / 72.0
MESH = pl.DeviceIdType.MESH


def kernel(
    sp_in, sn_in, rp_in, rn_in, cr_in, ab_in, cell_in, wav_in, rc_in, tr_in,
    out_s, out_r, out_i,
    F, YB, YC, ZL, ZR, PS, YPB, YPC, E, G, GE, D, DG, CA, CB, CC, INJ, LP, ST,
    sp, sn, rp, rn, cr, ab, cell, wav, rc, tr,
    send, recv, fetch,
):
    fetched = [
        pltpu.make_async_copy(src, dst, fetch.at[i])
        for i, (src, dst) in enumerate(
            (
                (sn_in, sn), (rn_in, rn), (sp_in, sp), (rp_in, rp), (cr_in, cr),
                (ab_in, ab), (cell_in, cell), (wav_in, wav), (rc_in, rc), (tr_in, tr),
            )
        )
    ]
    for c in fetched:
        c.start()
    tx, ty, tz = sn.shape
    nchunk = tx // REACH
    nx, ny, nz = (lax.axis_size(a) for a in ("gx", "gy", "gz"))
    ix, iy, iz = (lax.axis_index(a) for a in ("gx", "gy", "gz"))
    copies = []

    def exists(dx, dy, dz):
        ok = None
        for d, i, n in ((dx, ix, nx), (dy, iy, ny), (dz, iz, nz)):
            if d:
                here = (i + d >= 0) & (i + d < n)
                ok = here if ok is None else ok & here
        return ok

    def device(dx, dy, dz):
        return {
            a: i + d for a, i, d in (("gx", ix, dx), ("gy", iy, dy), ("gz", iz, dz)) if d
        }

    class Copy:
        def __init__(self, src, dst, direction):
            number = len(copies)
            self.desc = pltpu.make_async_remote_copy(
                src_ref=src,
                dst_ref=dst,
                send_sem=send.at[number],
                recv_sem=recv.at[number],
                device_id=device(*direction),
                device_id_type=MESH,
            )
            self.out = exists(*direction)
            self.into = exists(*(-d for d in direction))
            copies.append(self)
            pl.when(self.out)(lambda: self.desc.start())

        def wait(self):
            pl.when(self.into)(lambda: self.desc.wait_recv())

        def finish(self):
            pl.when(self.out)(lambda: self.desc.wait_send())

    lane = lax.broadcasted_iota(jnp.int32, (8, LANES), 1)
    sub_z = lax.broadcasted_iota(jnp.int32, (8, tz), 0)
    lane_z = lax.broadcasted_iota(jnp.int32, (8, tz), 1)
    even, odd = pl.ds(0, ty, 2), pl.ds(1, ty, 2)

    def each(low, high, body, unroll=1):
        def step(i, carry):
            body(i)
            return carry

        lax.fori_loop(low, high, step, 0, unroll=unroll)

    tiles = tz // LANES

    def weave(slot, x, a, b):
        for q in range(tiles):
            part = slice(q * LANES, (q + 1) * LANES)
            ST[slot, x, q, even, :] = a[:, part]
            ST[slot, x, q, odd, :] = b[:, part]
        return jnp.concatenate([ST[slot, x, q] for q in range(tiles)], axis=1)

    def unweave(x, v, at):
        for q in range(tiles):
            LP[x, q] = v[:, q * LANES : (q + 1) * LANES]
        return [
            jnp.concatenate([LP[x, q, rows, :] for q in range(tiles)], axis=1) for rows in at
        ]

    def load_now(x):
        F[1, H + x] = weave(0, x, sn[x], rn[x])

    low_x, high_x = ix == 0, ix == nx - 1
    low_y, high_y = iy == 0, iy == ny - 1
    low_z, high_z = iz == 0, iz == nz - 1

    @pl.when(low_x)
    def _():
        for i in range(1, STEPS + 2):
            F[i, 0:H] = jnp.zeros((H, 8, tz), jnp.float32)

    @pl.when(high_x)
    def _():
        for i in range(1, STEPS + 2):
            F[i, H + tx : 2 * H + tx] = jnp.zeros((H, 8, tz), jnp.float32)

    for missing, buf, packed in ((low_y, YB, YPB), (high_y, YC, YPC)):

        @pl.when(missing)
        def _(buf=buf):
            buf[...] = jnp.zeros(buf.shape, jnp.float32)

        @pl.when(missing | low_x | high_x)
        def _(packed=packed):
            packed[...] = jnp.zeros(packed.shape, jnp.float32)

    for missing, buf in ((low_z, ZL), (high_z, ZR)):

        @pl.when(missing | low_x | high_x)
        def _(buf=buf):
            buf[...] = jnp.zeros(buf.shape, jnp.float32)

    signs = (-1, 1)
    around = [(s, 0, 0) for s in signs] + [(0, s, 0) for s in signs] + [(0, 0, s) for s in signs]
    around += [(s, r, 0) for s in signs for r in signs] + [(s, 0, r) for s in signs for r in signs]
    barrier = pltpu.get_barrier_semaphore()
    count = 0
    for direction in around:
        there = exists(*direction)
        count = count + there.astype(jnp.int32)

        @pl.when(there)
        def _(direction=direction):
            pl.semaphore_signal(
                barrier, inc=1, device_id=device(*direction), device_id_type=MESH
            )

    for c in fetched[:2]:
        c.wait()
    each(0, tx, load_now, unroll=4)
    pl.semaphore_wait(barrier, count)

    def send_x(f, low, high):
        left = Copy(
            F.at[f, H + low : H + high],
            F.at[f, H + tx + low : H + tx + high],
            (-1, 0, 0),
        )
        right = Copy(
            F.at[f, H + tx - high : H + tx - low],
            F.at[f, H - high : H - low],
            (1, 0, 0),
        )
        return left, right

    def send_y(f, c):
        own = F.at[f, H + c * REACH : H + (c + 1) * REACH]
        there = pl.ds(c * REACH, REACH)
        return (
            Copy(own, YB.at[f - 1, there], (0, 1, 0)),
            Copy(own, YC.at[f - 1, there], (0, -1, 0)),
        )

    def send_z(f, low, high, dx=0):
        rows = pl.ds(H + low, high - low)
        there = pl.ds(H + low - dx * tx, high - low)
        return (
            Copy(F.at[f, rows, :, pl.ds(tz - LANES, LANES)], ZL.at[f - 1, there], (dx, 0, 1)),
            Copy(F.at[f, rows, :, pl.ds(0, LANES)], ZR.at[f - 1, there], (dx, 0, -1)),
        )

    def send_rows(f, s):
        def pack(g):
            first, last = F[f, H + g * REACH], F[f, H + g * REACH]
            last = pltpu.roll(last, 2, 0)
            for j in range(1, REACH):
                row = F[f, H + g * REACH + j]
                here = sub_z // 2 == j
                first = jnp.where(here, pltpu.roll(row, 2 * j, 0), first)
                shift = (2 * j - 6) % 8
                last = jnp.where(here, pltpu.roll(row, shift, 0) if shift else row, last)
            PS[s, 0, g] = first
            PS[s, 1, g] = last

        each(0, nchunk, pack)
        groups = HALF // REACH
        done = []
        for dy, side, buf in ((1, 1, YPB), (-1, 0, YPC)):
            done.append(
                Copy(PS.at[s, side], buf.at[s, groups : groups + nchunk], (0, dy, 0))
            )
            done.append(
                Copy(
                    PS.at[s, side, 0:groups],
                    buf.at[s, groups + nchunk : 2 * groups + nchunk],
                    (-1, dy, 0),
                )
            )
            done.append(
                Copy(
                    PS.at[s, side, nchunk - groups : nchunk],
                    buf.at[s, 0:groups],
                    (1, dy, 0),
                )
            )
        return done

    order = [0] + [nchunk - 1] * (nchunk > 1) + list(range(1, nchunk - 1))
    xw, yw, zw = {}, {}, {}
    xw[1] = send_x(1, 0, REACH)
    for c in order:
        yw[1, c] = send_y(1, c)
        zw[1, c] = send_z(1, c * REACH, (c + 1) * REACH)

    x_start, y_start, z_start = ix * tx, iy * ty, iz * tz

    def load_rest(x):
        F[0, H + x] = weave(1, x, sp[x], rp[x])
        damping = ab[x].astype(jnp.float32) / 16.0
        inverse = 1.0 / (1.0 + damping)
        c2 = cr[x] * inverse
        a2 = 2.0 * inverse + (3.0 * centre_weight) * c2
        b2 = (damping - 1.0) * inverse
        CA[x] = weave(2, x, a2, a2)
        CB[x] = weave(3, x, b2, b2)
        CC[x] = weave(4, x, c2, c2)
        rows = x * 8 + lax.broadcasted_iota(jnp.int32, (8, rc.shape[1]), 0)
        y_of = rc[1:2, :] - y_start
        where = (rc[0:1, :] - x_start) * 8 + y_of * 2 + 1
        where = jnp.where((y_of >= 0) & (y_of < ty), where, -1)
        top = jnp.where(iz == 0, 1.0, 0.0)
        for t in range(STEPS):
            total = jnp.sum(
                jnp.where(rows == where, tr[t : t + 1, :], 0.0), axis=1, keepdims=True
            )
            INJ[t, x] = jnp.where(lane == 0, total * top, 0.0)

    for c in fetched[2:]:
        c.wait()
    each(0, tx, load_rest, unroll=2)
    point = jnp.where(
        (lane_z == cell[2] - z_start) & (sub_z == (cell[1] - y_start) * 2), 1.0, 0.0
    )
    source_x = cell[0] - x_start

    def swap(v):
        parity = lax.broadcasted_iota(jnp.int32, v.shape, 0) % 2
        return jnp.where(parity == 0, pltpu.roll(v, 7, 0), pltpu.roll(v, 1, 0))

    def prepare(s, f):
        for w in late[s]:
            w.wait()

        def swapped(x):
            G[s, x] = swap(F[f, x])

        each(0, tx + 2 * H, swapped, unroll=5)

        def edges(x):
            edge = jnp.where(lane < LANES // 2, ZR[f - 1, x], ZL[f - 1, x])
            E[s, x] = edge
            GE[s, x] = swap(edge)

        each(H - HALF, H + tx + HALF, edges, unroll=4)

        def unpack(g):
            above, below = YPC[s, g], YPB[s, g]
            for j in range(REACH):
                first = pltpu.roll(above, (8 - 2 * j) % 8, 0) if j else above
                shift = (6 - 2 * j) % 8
                other = pltpu.roll(below, shift, 0) if shift else below
                both = jnp.where(sub_z < 4, first, other)
                D[s, g * REACH + j] = both
                DG[s, g * REACH + j] = swap(both)

        each(0, (tx + 2 * HALF) // REACH, unpack)

    def advance(t, c):
        f = t + 1

        def body(j):
            x = c * REACH + j
            cur = F[f, H + x]
            below, above = YB[t, x], YC[t, x]
            edge = jnp.where(lane < LANES // 2, ZR[t, H + x], ZL[t, H + x])
            row = jnp.concatenate([cur, edge], axis=1)
            wide = tz + LANES
            total = None
            for k, w in ((1, W1), (2, W2), (3, W3), (4, W4)):
                part = F[f, H + x + k] + F[f, H + x - k]
                part = part + (pltpu.roll(row, k, 1) + pltpu.roll(row, wide - k, 1))[:, :tz]
                if k == 4:
                    part = part + (above + below)
                total = w * part if total is None else total + w * part

            def up(k):
                return jnp.where(sub_z < 2 * k, above, cur)

            def down(k):
                return jnp.where(sub_z >= 8 - 2 * k, below, cur)

            total = total + pltpu.roll(W1 * up(1) + W3 * down(3), 6, 0)
            total = total + pltpu.roll(W2 * (up(2) + down(2)), 4, 0)
            total = total + pltpu.roll(W3 * up(3) + W1 * down(1), 2, 0)
            new = CA[x] * cur + CB[x] * F[f - 1, H + x] + CC[x] * total
            new = new + point * (wav[t] * (source_x == x).astype(jnp.float32))
            F[f + 1, H + x] = new
            F[f + 1, H + x, :, 0:LANES] = new[:, 0:LANES] + INJ[t, x]

        each(0, REACH, body, unroll=2)

    late = {}
    snaps = [t + 2 for t in range(STEPS) if (t + 1) % EVERY == 0]
    for t in range(STEPS):
        f = t + 1
        nf = f + 1
        last = t == STEPS - 1
        for number, c in enumerate(order):
            if number == 0:
                xw[f][1].wait()
                if nchunk == 1:
                    xw[f][0].wait()
            if number == 1:
                xw[f][0].wait()
            for w in yw[f, c] + zw[f, c]:
                w.wait()
            advance(t, c)
            if not last:
                yw[nf, c] = send_y(nf, c)
                zw[nf, c] = send_z(nf, c * REACH, (c + 1) * REACH)
                if number == min(1, nchunk - 1):
                    xw[nf] = send_x(nf, 0, REACH)
        if nf in snaps:
            s = snaps.index(nf)
            late[s] = list(send_x(nf, 0 if last else REACH, H))
            if last:
                late[s] += send_z(nf, 0, tx)
            late[s] += send_rows(nf, s)
            late[s] += send_z(nf, 0, HALF, -1)
            late[s] += send_z(nf, tx - HALF, tx, 1)
        elif snaps[0] < nf:
            prepare(0, snaps[0])

    def out_fields(x):
        out_s[x], out_r[x] = unweave(x, F[STEPS + 1, H + x], (even, odd))

    each(0, tx, out_fields, unroll=4)

    nsnap = len(snaps)
    for s in range(1, nsnap):
        prepare(s, snaps[s])

    def image(m, keep_even, keep_odd):
        def product(x):
            a, b = HALF + x - m, HALF + x + m
            total = F[snaps[0], a] * G[0, b]
            for s in range(1, nsnap):
                total = total + F[snaps[s], a] * G[s, b]
            return total

        def halo(x):
            a, b = H + x - m, H + x + m
            edge = E[0, a] * GE[0, b]
            for s in range(1, nsnap):
                edge = edge + E[s, a] * GE[s, b]
            a, b = HALF + x - m, HALF + x + m
            side = D[0, a] * DG[0, b]
            for s in range(1, nsnap):
                side = side + D[s, a] * DG[s, b]
            return edge, side

        before, centre = product(0), product(1)
        for x in range(tx):
            after = product(x + 2)
            edge, side = halo(x)
            row = jnp.concatenate([centre, edge], axis=1)
            wide = tz + LANES
            near = (pltpu.roll(row, 1, 1) + pltpu.roll(row, wide - 1, 1))[:, :tz]
            near = near + (before + after)
            near = near + pltpu.roll(jnp.where(sub_z < 2, side, centre), 6, 0)
            near = near + pltpu.roll(jnp.where(sub_z >= 6, side, centre), 2, 0)
            plus, minus = unweave(x, 6.0 * centre - near, (even, odd))
            if keep_even:
                out_i[HALF + m, x] = plus.astype(jnp.bfloat16)
            if keep_odd:
                out_i[HALF - m, x] = minus.astype(jnp.bfloat16)
            before, centre = centre, after

    image(0, True, False)
    each(1, HALF, lambda m: image(m, True, True))
    image(HALF, False, True)
    for c in copies:
        c.finish()


def local(
    source_prev,
    source_now,
    receiver_prev,
    receiver_now,
    courant,
    absorbing,
    source_cell,
    wavelet,
    receiver_cells,
    traces,
):
    tx, ty, tz = courant.shape
    nsnap = STEPS // EVERY
    nchunk = tx // REACH
    groups = (tx + 2 * HALF) // REACH
    f32 = jnp.float32
    vmem = pl.BlockSpec(memory_space=pltpu.VMEM)
    number = STEPS * (2 + 4 * nchunk) + nsnap * 14
    V = pltpu.VMEM
    return pl.pallas_call(
        kernel,
        out_shape=(
            jax.ShapeDtypeStruct((tx, ty, tz), f32),
            jax.ShapeDtypeStruct((tx, ty, tz), f32),
            jax.ShapeDtypeStruct((LAGS, tx, ty, tz), jnp.bfloat16),
        ),
        in_specs=[pl.BlockSpec(memory_space=pltpu.HBM)] * 10,
        out_specs=(vmem, vmem, vmem),
        scratch_shapes=[
            V((STEPS + 2, tx + 2 * H, 8, tz), f32),
            V((STEPS, tx, 8, tz), f32),
            V((STEPS, tx, 8, tz), f32),
            V((STEPS + 1, tx + 2 * H, 8, LANES), f32),
            V((STEPS + 1, tx + 2 * H, 8, LANES), f32),
            V((nsnap, 2, nchunk, 8, tz), f32),
            V((nsnap, groups, 8, tz), f32),
            V((nsnap, groups, 8, tz), f32),
            V((nsnap, tx + 2 * H, 8, LANES), f32),
            V((nsnap, tx + 2 * H, 8, tz), f32),
            V((nsnap, tx + 2 * H, 8, LANES), f32),
            V((nsnap, tx + 2 * HALF, 8, tz), f32),
            V((nsnap, tx + 2 * HALF, 8, tz), f32),
            V((tx, 8, tz), f32),
            V((tx, 8, tz), f32),
            V((tx, 8, tz), f32),
            V((STEPS, tx, 8, LANES), f32),
            V((tx, tz // LANES, 8, LANES), f32),
            V((5, tx, tz // LANES, 8, LANES), f32),
            *[V((tx, ty, tz), f32) for _ in range(5)],
            V((tx, ty, tz), jnp.int32),
            pltpu.SMEM(source_cell.shape, jnp.int32),
            pltpu.SMEM(wavelet.shape, f32),
            V(receiver_cells.shape[::-1], jnp.int32),
            V(traces.shape, f32),
            pltpu.SemaphoreType.DMA((number,)),
            pltpu.SemaphoreType.DMA((number,)),
            pltpu.SemaphoreType.DMA((10,)),
        ],
        compiler_params=pltpu.CompilerParams(
            collective_id=0, has_side_effects=True, vmem_limit_bytes=40 * 2**20
        ),
    )(
        source_prev,
        source_now,
        receiver_prev,
        receiver_now,
        courant,
        absorbing,
        source_cell,
        wavelet,
        receiver_cells.T,
        traces,
    )


def solution(mesh):
    placed = (
        P(("shot", "gx"), "gy", "gz"),
        P(("shot", "gx"), "gy", "gz"),
        P(("shot", "gx"), "gy", "gz"),
        P(("shot", "gx"), "gy", "gz"),
        P("gx", "gy", "gz"),
        P("gx", "gy", "gz"),
        P("shot"),
        P("shot"),
        P("shot", None),
        P(None, "shot"),
    )
    return jax.shard_map(
        local,
        mesh=mesh,
        in_specs=placed,
        out_specs=(
            P(("shot", "gx"), "gy", "gz"),
            P(("shot", "gx"), "gy", "gz"),
            P(None, ("shot", "gx"), "gy", "gz"),
        ),
        check_vma=False,
    )
```

```python
import functools
import jax
import jax.numpy as jnp
from jax import lax
from jax.experimental import pallas as pl
from jax.experimental.pallas import tpu as pltpu
from jax.sharding import PartitionSpec as P

LAGS = 16
STEPS = 4
EVERY = 2
HALF = LAGS // 2
H = HALF + 1
REACH = 4
LANES = 128

W1, W2, W3, W4 = (8.0 / 5.0, -1.0 / 5.0, 8.0 / 315.0, -1.0 / 560.0)
centre_weight = -205.0 / 72.0
MESH = pl.DeviceIdType.MESH


def kernel(
    sp_in, sn_in, rp_in, rn_in, cr_in, ab_in, cell_in, wav_in, rc_in, tr_in,
    out_s, out_r, out_i,
    F, YB, YC, ZL, ZR, PS, YPB, YPC, E, G, GE, D, DG, CA, CB, CC, INJ, LP, ST,
    sp, sn, rp, rn, cr, ab, cell, wav, rc, tr,
    send, recv, fetch,
):
    fetched = [
        pltpu.make_async_copy(src, dst, fetch.at[i])
        for i, (src, dst) in enumerate(
            (
                (sn_in, sn), (rn_in, rn), (sp_in, sp), (rp_in, rp), (cr_in, cr),
                (ab_in, ab), (cell_in, cell), (wav_in, wav), (rc_in, rc), (tr_in, tr),
            )
        )
    ]
    for c in fetched:
        c.start()
    tx, ty, tz = sn.shape
    nchunk = tx // REACH
    nx, ny, nz = (lax.axis_size(a) for a in ("gx", "gy", "gz"))
    ix, iy, iz = (lax.axis_index(a) for a in ("gx", "gy", "gz"))
    copies = []

    def exists(dx, dy, dz):
        ok = None
        for d, i, n in ((dx, ix, nx), (dy, iy, ny), (dz, iz, nz)):
            if d:
                here = (i + d >= 0) & (i + d < n)
                ok = here if ok is None else ok & here
        return ok

    def device(dx, dy, dz):
        return {
            a: i + d for a, i, d in (("gx", ix, dx), ("gy", iy, dy), ("gz", iz, dz)) if d
        }

    class Copy:
        def __init__(self, src, dst, direction):
            number = len(copies)
            self.desc = pltpu.make_async_remote_copy(
                src_ref=src,
                dst_ref=dst,
                send_sem=send.at[number],
                recv_sem=recv.at[number],
                device_id=device(*direction),
                device_id_type=MESH,
            )
            self.out = exists(*direction)
            self.into = exists(*(-d for d in direction))
            copies.append(self)
            pl.when(self.out)(lambda: self.desc.start())

        def wait(self):
            pl.when(self.into)(lambda: self.desc.wait_recv())

        def finish(self):
            pl.when(self.out)(lambda: self.desc.wait_send())

    lane = lax.broadcasted_iota(jnp.int32, (8, LANES), 1)
    sub_z = lax.broadcasted_iota(jnp.int32, (8, tz), 0)
    lane_z = lax.broadcasted_iota(jnp.int32, (8, tz), 1)
    even, odd = pl.ds(0, ty, 2), pl.ds(1, ty, 2)

    def each(low, high, body, unroll=1):
        def step(i, carry):
            body(i)
            return carry

        lax.fori_loop(low, high, step, 0, unroll=unroll)

    tiles = tz // LANES

    def weave(slot, x, a, b):
        for q in range(tiles):
            part = slice(q * LANES, (q + 1) * LANES)
            ST[slot, x, q, even, :] = a[:, part]
            ST[slot, x, q, odd, :] = b[:, part]
        return jnp.concatenate([ST[slot, x, q] for q in range(tiles)], axis=1)

    def unweave(x, v, at):
        for q in range(tiles):
            LP[x, q] = v[:, q * LANES : (q + 1) * LANES]
        return [
            jnp.concatenate([LP[x, q, rows, :] for q in range(tiles)], axis=1) for rows in at
        ]

    def load_now(x):
        F[1, H + x] = weave(0, x, sn[x], rn[x])

    low_x, high_x = ix == 0, ix == nx - 1
    low_y, high_y = iy == 0, iy == ny - 1
    low_z, high_z = iz == 0, iz == nz - 1

    @pl.when(low_x)
    def _():
        for i in range(1, STEPS + 2):
            F[i, 0:H] = jnp.zeros((H, 8, tz), jnp.float32)

    @pl.when(high_x)
    def _():
        for i in range(1, STEPS + 2):
            F[i, H + tx : 2 * H + tx] = jnp.zeros((H, 8, tz), jnp.float32)

    for missing, buf, packed in ((low_y, YB, YPB), (high_y, YC, YPC)):

        @pl.when(missing)
        def _(buf=buf):
            buf[...] = jnp.zeros(buf.shape, jnp.float32)

        @pl.when(missing | low_x | high_x)
        def _(packed=packed):
            packed[...] = jnp.zeros(packed.shape, jnp.float32)

    for missing, buf in ((low_z, ZL), (high_z, ZR)):

        @pl.when(missing | low_x | high_x)
        def _(buf=buf):
            buf[...] = jnp.zeros(buf.shape, jnp.float32)

    signs = (-1, 1)
    around = [(s, 0, 0) for s in signs] + [(0, s, 0) for s in signs] + [(0, 0, s) for s in signs]
    around += [(s, r, 0) for s in signs for r in signs] + [(s, 0, r) for s in signs for r in signs]
    barrier = pltpu.get_barrier_semaphore()
    count = 0
    for direction in around:
        there = exists(*direction)
        count = count + there.astype(jnp.int32)

        @pl.when(there)
        def _(direction=direction):
            pl.semaphore_signal(
                barrier, inc=1, device_id=device(*direction), device_id_type=MESH
            )

    for c in fetched[:2]:
        c.wait()
    each(0, tx, load_now, unroll=4)
    pl.semaphore_wait(barrier, count)

    def send_x(f, low, high):
        left = Copy(
            F.at[f, H + low : H + high],
            F.at[f, H + tx + low : H + tx + high],
            (-1, 0, 0),
        )
        right = Copy(
            F.at[f, H + tx - high : H + tx - low],
            F.at[f, H - high : H - low],
            (1, 0, 0),
        )
        return left, right

    def send_y(f, c):
        own = F.at[f, H + c * REACH : H + (c + 1) * REACH]
        there = pl.ds(c * REACH, REACH)
        return (
            Copy(own, YB.at[f - 1, there], (0, 1, 0)),
            Copy(own, YC.at[f - 1, there], (0, -1, 0)),
        )

    def send_z(f, low, high, dx=0):
        rows = pl.ds(H + low, high - low)
        there = pl.ds(H + low - dx * tx, high - low)
        return (
            Copy(F.at[f, rows, :, pl.ds(tz - LANES, LANES)], ZL.at[f - 1, there], (dx, 0, 1)),
            Copy(F.at[f, rows, :, pl.ds(0, LANES)], ZR.at[f - 1, there], (dx, 0, -1)),
        )

    groups = HALF // REACH

    def gather(rows, first):
        packed = None
        for k in range(REACH):
            row = rows[k]
            shift = (2 * k - first) % 8
            row = pltpu.roll(row, shift, 0) if shift else row
            packed = row if packed is None else jnp.where(sub_z // 2 == k, row, packed)
        return packed

    def pass_on(src, buf, s, g, dy):
        done = []
        if g < groups:
            done.append(Copy(src, buf.at[s, groups + nchunk + g], (-1, dy, 0)))
        if g >= nchunk - groups:
            done.append(Copy(src, buf.at[s, g - (nchunk - groups)], (1, dy, 0)))
        return done

    def send_rows(f, s, g):
        rows = [F[f, H + g * REACH + k] for k in range(REACH)]
        PS[s, 0, g] = gather(rows, 0)
        PS[s, 1, g] = gather(rows, 6)
        done = []
        for dy, side, buf in ((1, 1, YPB), (-1, 0, YPC)):
            src = PS.at[s, side, g]
            done.append(Copy(src, buf.at[s, groups + g], (0, dy, 0)))
            done += pass_on(src, buf, s, g, dy)
        return done

    def relay_rows(f, s, g):
        done = []
        for src, buf, first in ((YB, YPB, 6), (YC, YPC, 0)):
            buf[s, groups + g] = gather(
                [src[f - 1, g * REACH + k] for k in range(REACH)], first
            )
            done += pass_on(buf.at[s, groups + g], buf, s, g, 0)
        return done

    order = [0] + [nchunk - 1] * (nchunk > 1) + list(range(1, nchunk - 1))
    xw, yw, zw = {}, {}, {}
    xw[1] = send_x(1, 0, REACH)
    for c in order:
        yw[1, c] = send_y(1, c)
        zw[1, c] = send_z(1, c * REACH, (c + 1) * REACH)

    x_start, y_start, z_start = ix * tx, iy * ty, iz * tz

    def load_rest(x):
        F[0, H + x] = weave(1, x, sp[x], rp[x])
        damping = ab[x].astype(jnp.float32) / 16.0
        inverse = 1.0 / (1.0 + damping)
        c2 = cr[x] * inverse
        a2 = 2.0 * inverse + (3.0 * centre_weight) * c2
        b2 = (damping - 1.0) * inverse
        CA[x] = weave(2, x, a2, a2)
        CB[x] = weave(3, x, b2, b2)
        CC[x] = weave(4, x, c2, c2)
        rows = x * 8 + lax.broadcasted_iota(jnp.int32, (8, rc.shape[1]), 0)
        y_of = rc[1:2, :] - y_start
        where = (rc[0:1, :] - x_start) * 8 + y_of * 2 + 1
        where = jnp.where((y_of >= 0) & (y_of < ty), where, -1)
        top = jnp.where(iz == 0, 1.0, 0.0)
        for t in range(STEPS):
            total = jnp.sum(
                jnp.where(rows == where, tr[t : t + 1, :], 0.0), axis=1, keepdims=True
            )
            INJ[t, x] = jnp.where(lane == 0, total * top, 0.0)

    for c in fetched[2:]:
        c.wait()
    each(0, tx, load_rest, unroll=2)
    point = jnp.where(
        (lane_z == cell[2] - z_start) & (sub_z == (cell[1] - y_start) * 2), 1.0, 0.0
    )
    source_x = cell[0] - x_start

    def swap(v):
        parity = lax.broadcasted_iota(jnp.int32, v.shape, 0) % 2
        return jnp.where(parity == 0, pltpu.roll(v, 7, 0), pltpu.roll(v, 1, 0))

    def prepare(s, f):
        for w in late[s]:
            w.wait()

        def swapped(x):
            G[s, x] = swap(F[f, x])

        each(0, tx + 2 * H, swapped, unroll=5)

        def edges(x):
            edge = jnp.where(lane < LANES // 2, ZR[f - 1, x], ZL[f - 1, x])
            E[s, x] = edge
            GE[s, x] = swap(edge)

        each(H - HALF, H + tx + HALF, edges, unroll=4)

        def unpack(g):
            above, below = YPC[s, g], YPB[s, g]
            for j in range(REACH):
                first = pltpu.roll(above, (8 - 2 * j) % 8, 0) if j else above
                shift = (6 - 2 * j) % 8
                other = pltpu.roll(below, shift, 0) if shift else below
                both = jnp.where(sub_z < 4, first, other)
                D[s, g * REACH + j] = both
                DG[s, g * REACH + j] = swap(both)

        each(0, (tx + 2 * HALF) // REACH, unpack)

    def advance(t, c):
        f = t + 1

        def body(j):
            x = c * REACH + j
            cur = F[f, H + x]
            below, above = YB[t, x], YC[t, x]
            edge = jnp.where(lane < LANES // 2, ZR[t, H + x], ZL[t, H + x])
            row = jnp.concatenate([cur, edge], axis=1)
            wide = tz + LANES
            total = None
            for k, w in ((1, W1), (2, W2), (3, W3), (4, W4)):
                part = F[f, H + x + k] + F[f, H + x - k]
                part = part + (pltpu.roll(row, k, 1) + pltpu.roll(row, wide - k, 1))[:, :tz]
                if k == 4:
                    part = part + (above + below)
                total = w * part if total is None else total + w * part

            def up(k):
                return jnp.where(sub_z < 2 * k, above, cur)

            def down(k):
                return jnp.where(sub_z >= 8 - 2 * k, below, cur)

            total = total + pltpu.roll(W1 * up(1) + W3 * down(3), 6, 0)
            total = total + pltpu.roll(W2 * (up(2) + down(2)), 4, 0)
            total = total + pltpu.roll(W3 * up(3) + W1 * down(1), 2, 0)
            new = CA[x] * cur + CB[x] * F[f - 1, H + x] + CC[x] * total
            new = new + point * (wav[t] * (source_x == x).astype(jnp.float32))
            F[f + 1, H + x] = new
            F[f + 1, H + x, :, 0:LANES] = new[:, 0:LANES] + INJ[t, x]

        each(0, REACH, body, unroll=REACH)

    late = {}
    snaps = [t + 2 for t in range(STEPS) if (t + 1) % EVERY == 0]
    for t in range(STEPS):
        f = t + 1
        nf = f + 1
        last = t == STEPS - 1
        for number, c in enumerate(order):
            if number == 0:
                xw[f][1].wait()
                if nchunk == 1:
                    xw[f][0].wait()
            if number == 1:
                xw[f][0].wait()
            for w in yw[f, c] + zw[f, c]:
                w.wait()
            advance(t, c)
            if not last:
                yw[nf, c] = send_y(nf, c)
                zw[nf, c] = send_z(nf, c * REACH, (c + 1) * REACH)
                if number == min(1, nchunk - 1):
                    xw[nf] = send_x(nf, 0, REACH)
            elif nf in snaps:
                late.setdefault(snaps.index(nf), []).extend(send_rows(nf, snaps.index(nf), c))
            if f in snaps:
                late[snaps.index(f)] += relay_rows(f, snaps.index(f), c)
        if nf in snaps:
            s = snaps.index(nf)
            waits = late.setdefault(s, [])
            waits += send_x(nf, 0 if last else REACH, H)
            if last:
                waits += send_z(nf, 0, tx)
            waits += send_z(nf, 0, HALF, -1)
            waits += send_z(nf, tx - HALF, tx, 1)

    for s, f in enumerate(snaps[:-1]):
        prepare(s, f)

    def out_fields(x):
        out_s[x], out_r[x] = unweave(x, F[STEPS + 1, H + x], (even, odd))

    each(0, tx, out_fields, unroll=4)

    nsnap = len(snaps)
    prepare(nsnap - 1, snaps[-1])

    def image(m, keep_even, keep_odd):
        def product(x):
            a, b = HALF + x - m, HALF + x + m
            total = F[snaps[0], a] * G[0, b]
            for s in range(1, nsnap):
                total = total + F[snaps[s], a] * G[s, b]
            return total

        def halo(x):
            a, b = H + x - m, H + x + m
            edge = E[0, a] * GE[0, b]
            for s in range(1, nsnap):
                edge = edge + E[s, a] * GE[s, b]
            a, b = HALF + x - m, HALF + x + m
            side = D[0, a] * DG[0, b]
            for s in range(1, nsnap):
                side = side + D[s, a] * DG[s, b]
            return edge, side

        before, centre = product(0), product(1)
        for x in range(tx):
            after = product(x + 2)
            edge, side = halo(x)
            row = jnp.concatenate([centre, edge], axis=1)
            wide = tz + LANES
            near = (pltpu.roll(row, 1, 1) + pltpu.roll(row, wide - 1, 1))[:, :tz]
            near = near + (before + after)
            near = near + pltpu.roll(jnp.where(sub_z < 2, side, centre), 6, 0)
            near = near + pltpu.roll(jnp.where(sub_z >= 6, side, centre), 2, 0)
            plus, minus = unweave(x, 6.0 * centre - near, (even, odd))
            if keep_even:
                out_i[HALF + m, x] = plus.astype(jnp.bfloat16)
            if keep_odd:
                out_i[HALF - m, x] = minus.astype(jnp.bfloat16)
            before, centre = centre, after

    image(0, True, False)
    each(1, HALF, lambda m: image(m, True, True))
    image(HALF, False, True)
    for c in copies:
        c.finish()


def local(
    source_prev,
    source_now,
    receiver_prev,
    receiver_now,
    courant,
    absorbing,
    source_cell,
    wavelet,
    receiver_cells,
    traces,
):
    tx, ty, tz = courant.shape
    nsnap = STEPS // EVERY
    nchunk = tx // REACH
    groups = (tx + 2 * HALF) // REACH
    f32 = jnp.float32
    vmem = pl.BlockSpec(memory_space=pltpu.VMEM)
    number = STEPS * (2 + 4 * nchunk) + nsnap * 20
    V = pltpu.VMEM
    return pl.pallas_call(
        kernel,
        out_shape=(
            jax.ShapeDtypeStruct((tx, ty, tz), f32),
            jax.ShapeDtypeStruct((tx, ty, tz), f32),
            jax.ShapeDtypeStruct((LAGS, tx, ty, tz), jnp.bfloat16),
        ),
        in_specs=[pl.BlockSpec(memory_space=pltpu.HBM)] * 10,
        out_specs=(vmem, vmem, vmem),
        scratch_shapes=[
            V((STEPS + 2, tx + 2 * H, 8, tz), f32),
            V((STEPS, tx, 8, tz), f32),
            V((STEPS, tx, 8, tz), f32),
            V((STEPS + 1, tx + 2 * H, 8, LANES), f32),
            V((STEPS + 1, tx + 2 * H, 8, LANES), f32),
            V((nsnap, 2, nchunk, 8, tz), f32),
            V((nsnap, groups, 8, tz), f32),
            V((nsnap, groups, 8, tz), f32),
            V((nsnap, tx + 2 * H, 8, LANES), f32),
            V((nsnap, tx + 2 * H, 8, tz), f32),
            V((nsnap, tx + 2 * H, 8, LANES), f32),
            V((nsnap, tx + 2 * HALF, 8, tz), f32),
            V((nsnap, tx + 2 * HALF, 8, tz), f32),
            V((tx, 8, tz), f32),
            V((tx, 8, tz), f32),
            V((tx, 8, tz), f32),
            V((STEPS, tx, 8, LANES), f32),
            V((tx, tz // LANES, 8, LANES), f32),
            V((5, tx, tz // LANES, 8, LANES), f32),
            *[V((tx, ty, tz), f32) for _ in range(5)],
            V((tx, ty, tz), jnp.int32),
            pltpu.SMEM(source_cell.shape, jnp.int32),
            pltpu.SMEM(wavelet.shape, f32),
            V(receiver_cells.shape[::-1], jnp.int32),
            V(traces.shape, f32),
            pltpu.SemaphoreType.DMA((number,)),
            pltpu.SemaphoreType.DMA((number,)),
            pltpu.SemaphoreType.DMA((10,)),
        ],
        compiler_params=pltpu.CompilerParams(
            collective_id=0, has_side_effects=True, vmem_limit_bytes=63 * 2**20
        ),
    )(
        source_prev,
        source_now,
        receiver_prev,
        receiver_now,
        courant,
        absorbing,
        source_cell,
        wavelet,
        receiver_cells.T,
        traces,
    )


def solution(mesh):
    placed = (
        P(("shot", "gx"), "gy", "gz"),
        P(("shot", "gx"), "gy", "gz"),
        P(("shot", "gx"), "gy", "gz"),
        P(("shot", "gx"), "gy", "gz"),
        P("gx", "gy", "gz"),
        P("gx", "gy", "gz"),
        P("shot"),
        P("shot"),
        P("shot", None),
        P(None, "shot"),
    )
    return jax.shard_map(
        local,
        mesh=mesh,
        in_specs=placed,
        out_specs=(
            P(("shot", "gx"), "gy", "gz"),
            P(("shot", "gx"), "gy", "gz"),
            P(None, ("shot", "gx"), "gy", "gz"),
        ),
        check_vma=False,
    )
```

```python
import functools
import jax
import jax.numpy as jnp
from jax import lax
from jax.experimental import pallas as pl
from jax.experimental.pallas import tpu as pltpu
from jax.sharding import PartitionSpec as P

LAGS = 16
STEPS = 4
EVERY = 2
HALF = LAGS // 2
H = HALF + 1
REACH = 4
LANES = 128

W1, W2, W3, W4 = (8.0 / 5.0, -1.0 / 5.0, 8.0 / 315.0, -1.0 / 560.0)
centre_weight = -205.0 / 72.0
MESH = pl.DeviceIdType.MESH


def kernel(
    sp_in, sn_in, rp_in, rn_in, cr_in, ab_in, cell_in, wav_in, rc_in, tr_in,
    to_s, to_r, to_i,
    out_s, out_r, out_i,
    F, YB, YC, ZL, ZR, PS, YPB, YPC, E, G, GE, D, DG, CA, CB, CC, INJ, LP, ST,
    sp, sn, rp, rn, cr, ab, cell, wav, rc, tr,
    send, recv, fetch, leave,
):
    tx, ty, tz = sn.shape
    nchunk = tx // REACH
    snaps = [t + 2 for t in range(STEPS) if (t + 1) % EVERY == 0]
    nsnap = len(snaps)
    nx, ny, nz = (lax.axis_size(a) for a in ("gx", "gy", "gz"))
    ix, iy, iz = (lax.axis_index(a) for a in ("gx", "gy", "gz"))
    copies = []

    def exists(dx, dy, dz):
        ok = None
        for d, i, n in ((dx, ix, nx), (dy, iy, ny), (dz, iz, nz)):
            if d:
                here = (i + d >= 0) & (i + d < n)
                ok = here if ok is None else ok & here
        return ok

    def device(dx, dy, dz):
        return {
            a: i + d for a, i, d in (("gx", ix, dx), ("gy", iy, dy), ("gz", iz, dz)) if d
        }

    class Copy:
        def __init__(self, src, dst, direction):
            number = len(copies)
            self.desc = pltpu.make_async_remote_copy(
                src_ref=src,
                dst_ref=dst,
                send_sem=send.at[number],
                recv_sem=recv.at[number],
                device_id=device(*direction),
                device_id_type=MESH,
            )
            self.out = exists(*direction)
            self.into = exists(*(-d for d in direction))
            copies.append(self)
            pl.when(self.out)(lambda: self.desc.start())

        def wait(self):
            pl.when(self.into)(lambda: self.desc.wait_recv())

        def finish(self):
            pl.when(self.out)(lambda: self.desc.wait_send())

    lane = lax.broadcasted_iota(jnp.int32, (8, LANES), 1)
    sub_z = lax.broadcasted_iota(jnp.int32, (8, tz), 0)
    lane_z = lax.broadcasted_iota(jnp.int32, (8, tz), 1)
    even, odd = pl.ds(0, ty, 2), pl.ds(1, ty, 2)

    def each(low, high, body, unroll=1):
        def step(i, carry):
            body(i)
            return carry

        lax.fori_loop(low, high, step, 0, unroll=unroll)

    tiles = tz // LANES

    def weave(slot, x, a, b):
        for q in range(tiles):
            part = slice(q * LANES, (q + 1) * LANES)
            ST[slot, x, q, even, :] = a[:, part]
            ST[slot, x, q, odd, :] = b[:, part]
        return jnp.concatenate([ST[slot, x, q] for q in range(tiles)], axis=1)

    def unweave(x, v, at):
        for q in range(tiles):
            LP[x, q] = v[:, q * LANES : (q + 1) * LANES]
        return [
            jnp.concatenate([LP[x, q, rows, :] for q in range(tiles)], axis=1) for rows in at
        ]

    def load_now(x):
        F[1, H + x] = weave(0, x, sn[x], rn[x])

    low_x, high_x = ix == 0, ix == nx - 1
    low_y, high_y = iy == 0, iy == ny - 1
    low_z, high_z = iz == 0, iz == nz - 1

    signs = (-1, 1)
    around = [(s, 0, 0) for s in signs] + [(0, s, 0) for s in signs] + [(0, 0, s) for s in signs]
    around += [(s, r, 0) for s in signs for r in signs] + [(s, 0, r) for s in signs for r in signs]
    barrier = pltpu.get_barrier_semaphore()
    count = 0
    for direction in around:
        there = exists(*direction)
        count = count + there.astype(jnp.int32)

        @pl.when(there)
        def _(direction=direction):
            pl.semaphore_signal(
                barrier, inc=1, device_id=device(*direction), device_id_type=MESH
            )

    fetched = [
        pltpu.make_async_copy(src, dst, fetch.at[i])
        for i, (src, dst) in enumerate(
            (
                (sn_in, sn), (rn_in, rn), (sp_in, sp), (rp_in, rp), (cr_in, cr),
                (ab_in, ab), (cell_in, cell), (wav_in, wav), (rc_in, rc), (tr_in, tr),
            )
        )
    ]
    for c in fetched:
        c.start()
    for c in fetched[:2]:
        c.wait()
    each(0, tx, load_now, unroll=4)
    pl.semaphore_wait(barrier, count)

    def send_x(f, low, high):
        left = Copy(
            F.at[f, H + low : H + high],
            F.at[f, H + tx + low : H + tx + high],
            (-1, 0, 0),
        )
        right = Copy(
            F.at[f, H + tx - high : H + tx - low],
            F.at[f, H - high : H - low],
            (1, 0, 0),
        )
        return left, right

    def send_x_chunk(f, c):
        done = []
        low, high = c * REACH, min((c + 1) * REACH, H)
        if low < high:
            done.append(
                Copy(F.at[f, H + low : H + high], F.at[f, H + tx + low : H + tx + high], (-1, 0, 0))
            )
        low, high = max(c * REACH, tx - H), (c + 1) * REACH
        if low < high:
            done.append(
                Copy(F.at[f, H + low : H + high], F.at[f, H + low - tx : H + high - tx], (1, 0, 0))
            )
        return done

    def send_y(f, c):
        own = F.at[f, H + c * REACH : H + (c + 1) * REACH]
        there = pl.ds(c * REACH, REACH)
        return (
            Copy(own, YB.at[f - 1, there], (0, 1, 0)),
            Copy(own, YC.at[f - 1, there], (0, -1, 0)),
        )

    def send_z(f, low, high, dx=0):
        rows = pl.ds(H + low, high - low)
        there = pl.ds(H + low - dx * tx, high - low)
        return (
            Copy(F.at[f, rows, :, pl.ds(tz - LANES, LANES)], ZL.at[f - 1, there], (dx, 0, 1)),
            Copy(F.at[f, rows, :, pl.ds(0, LANES)], ZR.at[f - 1, there], (dx, 0, -1)),
        )

    groups = HALF // REACH

    def gather(rows, first):
        packed = None
        for k in range(REACH):
            row = rows[k]
            shift = (2 * k - first) % 8
            row = pltpu.roll(row, shift, 0) if shift else row
            packed = row if packed is None else jnp.where(sub_z // 2 == k, row, packed)
        return packed

    def pass_on(src, buf, s, g, dy):
        done = []
        if g < groups:
            done.append(Copy(src, buf.at[s, groups + nchunk + g], (-1, dy, 0)))
        if g >= nchunk - groups:
            done.append(Copy(src, buf.at[s, g - (nchunk - groups)], (1, dy, 0)))
        return done

    def send_rows(f, s, g):
        rows = [F[f, H + g * REACH + k] for k in range(REACH)]
        PS[s, 0, g] = gather(rows, 0)
        PS[s, 1, g] = gather(rows, 6)
        done = []
        for dy, side, buf in ((1, 1, YPB), (-1, 0, YPC)):
            src = PS.at[s, side, g]
            done.append(Copy(src, buf.at[s, groups + g], (0, dy, 0)))
            done += pass_on(src, buf, s, g, dy)
        return done

    def relay_rows(f, s, g):
        done = []
        for src, buf, first in ((YB, YPB, 6), (YC, YPC, 0)):
            buf[s, groups + g] = gather(
                [src[f - 1, g * REACH + k] for k in range(REACH)], first
            )
            done += pass_on(buf.at[s, groups + g], buf, s, g, 0)
        return done

    order = [0] + [nchunk - 1] * (nchunk > 1) + list(range(1, nchunk - 1))
    xw, yw, zw = {}, {}, {}
    xw[1] = send_x(1, 0, REACH)
    for c in order:
        yw[1, c] = send_y(1, c)
        zw[1, c] = send_z(1, c * REACH, (c + 1) * REACH)

    def zero(missing, *refs):
        @pl.when(missing)
        def _():
            for ref in refs:
                ref[...] = jnp.zeros(ref.shape, jnp.float32)

    low_rows, high_rows = pl.ds(0, H), pl.ds(H + tx, H)
    low_packs, high_packs = pl.ds(0, groups), pl.ds(groups + nchunk, groups)
    zero(low_x, *[F.at[i, low_rows] for i in range(1, STEPS + 2)])
    zero(high_x, *[F.at[i, high_rows] for i in range(1, STEPS + 2)])
    zero(low_y, YB, YPB)
    zero(high_y, YC, YPC)
    zero(low_z, ZL)
    zero(high_z, ZR)
    zero(low_x, *[b.at[snaps[s] - 1, low_rows] for b in (ZL, ZR) for s in range(nsnap)])
    zero(high_x, *[b.at[snaps[s] - 1, high_rows] for b in (ZL, ZR) for s in range(nsnap)])
    zero(low_x, *[b.at[s, low_packs] for b in (YPB, YPC) for s in range(nsnap)])
    zero(high_x, *[b.at[s, high_packs] for b in (YPB, YPC) for s in range(nsnap)])

    x_start, y_start, z_start = ix * tx, iy * ty, iz * tz

    def load_rest(x):
        F[0, H + x] = weave(1, x, sp[x], rp[x])
        damping = ab[x].astype(jnp.float32) / 16.0
        inverse = 1.0 / (1.0 + damping)
        c2 = cr[x] * inverse
        a2 = 2.0 * inverse + (3.0 * centre_weight) * c2
        b2 = (damping - 1.0) * inverse
        CA[x] = weave(2, x, a2, a2)
        CB[x] = weave(3, x, b2, b2)
        CC[x] = weave(4, x, c2, c2)
        rows = x * 8 + lax.broadcasted_iota(jnp.int32, (8, rc.shape[1]), 0)
        y_of = rc[1:2, :] - y_start
        where = (rc[0:1, :] - x_start) * 8 + y_of * 2 + 1
        where = jnp.where((y_of >= 0) & (y_of < ty), where, -1)
        top = jnp.where(iz == 0, 1.0, 0.0)
        for t in range(STEPS):
            total = jnp.sum(
                jnp.where(rows == where, tr[t : t + 1, :], 0.0), axis=1, keepdims=True
            )
            INJ[t, x] = jnp.where(lane == 0, total * top, 0.0)

    for c in fetched[2:]:
        c.wait()
    each(0, tx, load_rest, unroll=2)
    point = jnp.where(
        (lane_z == cell[2] - z_start) & (sub_z == (cell[1] - y_start) * 2), 1.0, 0.0
    )
    source_x = cell[0] - x_start

    def swap(v):
        parity = lax.broadcasted_iota(jnp.int32, v.shape, 0) % 2
        return jnp.where(parity == 0, pltpu.roll(v, 7, 0), pltpu.roll(v, 1, 0))

    def prepare(s, f):
        for w in late[s]:
            w.wait()

        def swapped(x):
            G[s, x] = swap(F[f, x])

        each(0, tx + 2 * H, swapped, unroll=5)

        def edges(x):
            edge = jnp.where(lane < LANES // 2, ZR[f - 1, x], ZL[f - 1, x])
            E[s, x] = edge
            GE[s, x] = swap(edge)

        each(H - HALF, H + tx + HALF, edges, unroll=4)

        def unpack(g):
            above, below = YPC[s, g], YPB[s, g]
            for j in range(REACH):
                first = pltpu.roll(above, (8 - 2 * j) % 8, 0) if j else above
                shift = (6 - 2 * j) % 8
                other = pltpu.roll(below, shift, 0) if shift else below
                both = jnp.where(sub_z < 4, first, other)
                D[s, g * REACH + j] = both
                DG[s, g * REACH + j] = swap(both)

        each(0, (tx + 2 * HALF) // REACH, unpack)

    def advance(t, c):
        f = t + 1

        def body(j):
            x = c * REACH + j
            cur = F[f, H + x]
            below, above = YB[t, x], YC[t, x]
            edge = jnp.where(lane < LANES // 2, ZR[t, H + x], ZL[t, H + x])
            row = jnp.concatenate([cur, edge], axis=1)
            wide = tz + LANES
            total = None
            for k, w in ((1, W1), (2, W2), (3, W3), (4, W4)):
                part = F[f, H + x + k] + F[f, H + x - k]
                part = part + (pltpu.roll(row, k, 1) + pltpu.roll(row, wide - k, 1))[:, :tz]
                if k == 4:
                    part = part + (above + below)
                total = w * part if total is None else total + w * part

            def up(k):
                return jnp.where(sub_z < 2 * k, above, cur)

            def down(k):
                return jnp.where(sub_z >= 8 - 2 * k, below, cur)

            total = total + pltpu.roll(W1 * up(1) + W3 * down(3), 6, 0)
            total = total + pltpu.roll(W2 * (up(2) + down(2)), 4, 0)
            total = total + pltpu.roll(W3 * up(3) + W1 * down(1), 2, 0)
            new = CA[x] * cur + CB[x] * F[f - 1, H + x] + CC[x] * total
            new = new + point * (wav[t] * (source_x == x).astype(jnp.float32))
            F[f + 1, H + x] = new
            F[f + 1, H + x, :, 0:LANES] = new[:, 0:LANES] + INJ[t, x]

        each(0, REACH, body, unroll=REACH)

    late = {}
    for t in range(STEPS):
        f = t + 1
        nf = f + 1
        last = t == STEPS - 1
        for number, c in enumerate(order):
            if number == 0:
                xw[f][1].wait()
                if nchunk == 1:
                    xw[f][0].wait()
            if number == 1:
                xw[f][0].wait()
            for w in yw[f, c] + zw[f, c]:
                w.wait()
            advance(t, c)
            if not last:
                yw[nf, c] = send_y(nf, c)
                zw[nf, c] = send_z(nf, c * REACH, (c + 1) * REACH)
                if number == min(1, nchunk - 1):
                    xw[nf] = send_x(nf, 0, REACH)
            elif nf in snaps:
                waits = late.setdefault(snaps.index(nf), [])
                waits += send_x_chunk(nf, c)
                waits += send_rows(nf, snaps.index(nf), c)
            if f in snaps:
                late[snaps.index(f)] += relay_rows(f, snaps.index(f), c)
        if nf in snaps:
            s = snaps.index(nf)
            waits = late.setdefault(s, [])
            if not last:
                waits += send_x(nf, REACH, H)
            else:
                waits += send_z(nf, 0, tx)
            waits += send_z(nf, 0, HALF, -1)
            waits += send_z(nf, tx - HALF, tx, 1)

    def out_fields(x):
        out_s[x], out_r[x] = unweave(x, F[STEPS + 1, H + x], (even, odd))

    each(0, tx, out_fields, unroll=4)
    leaving = [
        pltpu.make_async_copy(out_s, to_s, leave.at[LAGS]),
        pltpu.make_async_copy(out_r, to_r, leave.at[LAGS + 1]),
    ]
    for c in leaving:
        c.start()

    def lag_out(lag):
        return pltpu.make_async_copy(out_i.at[lag], to_i.at[lag], leave.at[lag])

    for s, f in enumerate(snaps):
        prepare(s, f)

    def image(m, keep_even, keep_odd):
        def product(x):
            a, b = HALF + x - m, HALF + x + m
            total = F[snaps[0], a] * G[0, b]
            for s in range(1, nsnap):
                total = total + F[snaps[s], a] * G[s, b]
            return total

        def halo(x):
            a, b = H + x - m, H + x + m
            edge = E[0, a] * GE[0, b]
            for s in range(1, nsnap):
                edge = edge + E[s, a] * GE[s, b]
            a, b = HALF + x - m, HALF + x + m
            side = D[0, a] * DG[0, b]
            for s in range(1, nsnap):
                side = side + D[s, a] * DG[s, b]
            return edge, side

        before, centre = product(0), product(1)
        for x in range(tx):
            after = product(x + 2)
            edge, side = halo(x)
            row = jnp.concatenate([centre, edge], axis=1)
            wide = tz + LANES
            near = (pltpu.roll(row, 1, 1) + pltpu.roll(row, wide - 1, 1))[:, :tz]
            near = near + (before + after)
            near = near + pltpu.roll(jnp.where(sub_z < 2, side, centre), 6, 0)
            near = near + pltpu.roll(jnp.where(sub_z >= 6, side, centre), 2, 0)
            plus, minus = unweave(x, 6.0 * centre - near, (even, odd))
            if keep_even:
                out_i[HALF + m, x] = plus.astype(jnp.bfloat16)
            if keep_odd:
                out_i[HALF - m, x] = minus.astype(jnp.bfloat16)
            before, centre = centre, after
        if keep_even:
            lag_out(HALF + m).start()
        if keep_odd:
            lag_out(HALF - m).start()

    image(0, True, False)
    each(1, HALF, lambda m: image(m, True, True))
    image(HALF, False, True)
    for c in copies:
        c.finish()
    for c in leaving:
        c.wait()
    each(0, LAGS, lambda lag: lag_out(lag).wait())


def deliver(s, r, i, out_s, out_r, out_i, sems):
    pairs = [(s, out_s), (r, out_r)]
    part = LAGS // 4
    pairs += [
        (i.at[k * part : (k + 1) * part], out_i.at[k * part : (k + 1) * part]) for k in range(4)
    ]
    moves = [pltpu.make_async_copy(a, b, sems.at[n]) for n, (a, b) in enumerate(pairs)]
    for c in moves:
        c.start()
    for c in moves:
        c.wait()


def local(
    source_prev,
    source_now,
    receiver_prev,
    receiver_now,
    courant,
    absorbing,
    source_cell,
    wavelet,
    receiver_cells,
    traces,
):
    tx, ty, tz = courant.shape
    nsnap = STEPS // EVERY
    nchunk = tx // REACH
    groups = (tx + 2 * HALF) // REACH
    f32 = jnp.float32
    number = STEPS * (2 + 4 * nchunk) + nsnap * 20
    V = pltpu.VMEM
    results = (
        jax.ShapeDtypeStruct((tx, ty, tz), f32),
        jax.ShapeDtypeStruct((tx, ty, tz), f32),
        jax.ShapeDtypeStruct((LAGS, tx, ty, tz), jnp.bfloat16),
    )
    far = pl.BlockSpec(memory_space=pltpu.HBM)
    moved = pl.pallas_call(
        kernel,
        out_shape=results,
        in_specs=[far] * 10,
        out_specs=(far, far, far),
        scratch_shapes=[
            V((tx, ty, tz), f32),
            V((tx, ty, tz), f32),
            V((LAGS, tx, ty, tz), jnp.bfloat16),
            V((STEPS + 2, tx + 2 * H, 8, tz), f32),
            V((STEPS, tx, 8, tz), f32),
            V((STEPS, tx, 8, tz), f32),
            V((STEPS + 1, tx + 2 * H, 8, LANES), f32),
            V((STEPS + 1, tx + 2 * H, 8, LANES), f32),
            V((nsnap, 2, nchunk, 8, tz), f32),
            V((nsnap, groups, 8, tz), f32),
            V((nsnap, groups, 8, tz), f32),
            V((nsnap, tx + 2 * H, 8, LANES), f32),
            V((nsnap, tx + 2 * H, 8, tz), f32),
            V((nsnap, tx + 2 * H, 8, LANES), f32),
            V((nsnap, tx + 2 * HALF, 8, tz), f32),
            V((nsnap, tx + 2 * HALF, 8, tz), f32),
            V((tx, 8, tz), f32),
            V((tx, 8, tz), f32),
            V((tx, 8, tz), f32),
            V((STEPS, tx, 8, LANES), f32),
            V((tx, tz // LANES, 8, LANES), f32),
            V((5, tx, tz // LANES, 8, LANES), f32),
            *[V((tx, ty, tz), f32) for _ in range(5)],
            V((tx, ty, tz), jnp.int32),
            pltpu.SMEM(source_cell.shape, jnp.int32),
            pltpu.SMEM(wavelet.shape, f32),
            V(receiver_cells.shape[::-1], jnp.int32),
            V(traces.shape, f32),
            pltpu.SemaphoreType.DMA((number,)),
            pltpu.SemaphoreType.DMA((number,)),
            pltpu.SemaphoreType.DMA((10,)),
            pltpu.SemaphoreType.DMA((LAGS + 2,)),
        ],
        compiler_params=pltpu.CompilerParams(
            collective_id=0, has_side_effects=True, vmem_limit_bytes=63 * 2**20
        ),
    )(
        source_prev,
        source_now,
        receiver_prev,
        receiver_now,
        courant,
        absorbing,
        source_cell,
        wavelet,
        receiver_cells.T,
        traces,
    )
    return pl.pallas_call(
        deliver,
        out_shape=results,
        in_specs=[far] * 3,
        out_specs=(far, far, far),
        scratch_shapes=[pltpu.SemaphoreType.DMA((6,))],
        compiler_params=pltpu.CompilerParams(vmem_limit_bytes=63 * 2**20),
    )(*moved)


def solution(mesh):
    placed = (
        P(("shot", "gx"), "gy", "gz"),
        P(("shot", "gx"), "gy", "gz"),
        P(("shot", "gx"), "gy", "gz"),
        P(("shot", "gx"), "gy", "gz"),
        P("gx", "gy", "gz"),
        P("gx", "gy", "gz"),
        P("shot"),
        P("shot"),
        P("shot", None),
        P(None, "shot"),
    )
    return jax.shard_map(
        local,
        mesh=mesh,
        in_specs=placed,
        out_specs=(
            P(("shot", "gx"), "gy", "gz"),
            P(("shot", "gx"), "gy", "gz"),
            P(None, ("shot", "gx"), "gy", "gz"),
        ),
        check_vma=False,
    )
```

```python
import functools
import jax
import jax.numpy as jnp
from jax import lax
from jax.experimental import pallas as pl
from jax.experimental.pallas import tpu as pltpu
from jax.sharding import PartitionSpec as P

LAGS = 16
STEPS = 4
EVERY = 2
HALF = LAGS // 2
H = HALF + 1
REACH = 4
LANES = 128

W1, W2, W3, W4 = (8.0 / 5.0, -1.0 / 5.0, 8.0 / 315.0, -1.0 / 560.0)
centre_weight = -205.0 / 72.0
MESH = pl.DeviceIdType.MESH


def kernel(
    sp_in, sn_in, rp_in, rn_in, cr_in, ab_in, cell_in, wav_in, rc_in, tr_in,
    to_s, to_r, to_i,
    out_s, out_r, out_i,
    F, YB, YC, ZL, ZR, PS, YPB, YPC, E, G, GE, D, DG, CA, CB, CC, INJ, LP, ST,
    sp, sn, rp, rn, cr, ab, cell, wav, rc, tr,
    send, recv, fetch, leave,
):
    tx, ty, tz = sn.shape
    nchunk = tx // REACH
    snaps = [t + 2 for t in range(STEPS) if (t + 1) % EVERY == 0]
    nsnap = len(snaps)
    nx, ny, nz = (lax.axis_size(a) for a in ("gx", "gy", "gz"))
    ix, iy, iz = (lax.axis_index(a) for a in ("gx", "gy", "gz"))
    copies = []

    def exists(dx, dy, dz):
        ok = None
        for d, i, n in ((dx, ix, nx), (dy, iy, ny), (dz, iz, nz)):
            if d:
                here = (i + d >= 0) & (i + d < n)
                ok = here if ok is None else ok & here
        return ok

    def device(dx, dy, dz):
        return {
            a: i + d for a, i, d in (("gx", ix, dx), ("gy", iy, dy), ("gz", iz, dz)) if d
        }

    class Copy:
        def __init__(self, src, dst, direction):
            number = len(copies)
            self.desc = pltpu.make_async_remote_copy(
                src_ref=src,
                dst_ref=dst,
                send_sem=send.at[number],
                recv_sem=recv.at[number],
                device_id=device(*direction),
                device_id_type=MESH,
            )
            self.out = exists(*direction)
            self.into = exists(*(-d for d in direction))
            copies.append(self)
            pl.when(self.out)(lambda: self.desc.start())

        def wait(self):
            pl.when(self.into)(lambda: self.desc.wait_recv())

        def finish(self):
            pl.when(self.out)(lambda: self.desc.wait_send())

    lane = lax.broadcasted_iota(jnp.int32, (8, LANES), 1)
    sub_z = lax.broadcasted_iota(jnp.int32, (8, tz), 0)
    lane_z = lax.broadcasted_iota(jnp.int32, (8, tz), 1)
    even, odd = pl.ds(0, ty, 2), pl.ds(1, ty, 2)

    def each(low, high, body, unroll=1):
        def step(i, carry):
            body(i)
            return carry

        lax.fori_loop(low, high, step, 0, unroll=unroll)

    tiles = tz // LANES

    def weave(slot, x, a, b):
        for q in range(tiles):
            part = slice(q * LANES, (q + 1) * LANES)
            ST[slot, x, q, even, :] = a[:, part]
            ST[slot, x, q, odd, :] = b[:, part]
        return jnp.concatenate([ST[slot, x, q] for q in range(tiles)], axis=1)

    def unweave(x, v, at):
        for q in range(tiles):
            LP[x, q] = v[:, q * LANES : (q + 1) * LANES]
        return [
            jnp.concatenate([LP[x, q, rows, :] for q in range(tiles)], axis=1) for rows in at
        ]

    def load_now(x):
        F[1, H + x] = weave(0, x, sn[x], rn[x])

    low_x, high_x = ix == 0, ix == nx - 1
    low_y, high_y = iy == 0, iy == ny - 1
    low_z, high_z = iz == 0, iz == nz - 1

    signs = (-1, 1)
    around = [(s, 0, 0) for s in signs] + [(0, s, 0) for s in signs] + [(0, 0, s) for s in signs]
    around += [(s, r, 0) for s in signs for r in signs] + [(s, 0, r) for s in signs for r in signs]
    barrier = pltpu.get_barrier_semaphore()
    count = 0
    for direction in around:
        there = exists(*direction)
        count = count + there.astype(jnp.int32)

        @pl.when(there)
        def _(direction=direction):
            pl.semaphore_signal(
                barrier, inc=1, device_id=device(*direction), device_id_type=MESH
            )

    fetched = [
        pltpu.make_async_copy(src, dst, fetch.at[i])
        for i, (src, dst) in enumerate(
            (
                (sn_in, sn), (rn_in, rn), (sp_in, sp), (rp_in, rp), (cr_in, cr),
                (ab_in, ab), (cell_in, cell), (wav_in, wav), (rc_in, rc), (tr_in, tr),
            )
        )
    ]
    for c in fetched:
        c.start()
    for c in fetched[:2]:
        c.wait()
    each(0, tx, load_now, unroll=4)
    pl.semaphore_wait(barrier, count)

    def send_x(f, low, high):
        left = Copy(
            F.at[f, H + low : H + high],
            F.at[f, H + tx + low : H + tx + high],
            (-1, 0, 0),
        )
        right = Copy(
            F.at[f, H + tx - high : H + tx - low],
            F.at[f, H - high : H - low],
            (1, 0, 0),
        )
        return left, right

    def send_x_chunk(f, c):
        done = []
        low, high = c * REACH, min((c + 1) * REACH, H)
        if low < high:
            done.append(
                Copy(F.at[f, H + low : H + high], F.at[f, H + tx + low : H + tx + high], (-1, 0, 0))
            )
        low, high = max(c * REACH, tx - H), (c + 1) * REACH
        if low < high:
            done.append(
                Copy(F.at[f, H + low : H + high], F.at[f, H + low - tx : H + high - tx], (1, 0, 0))
            )
        return done

    def send_y(f, c):
        own = F.at[f, H + c * REACH : H + (c + 1) * REACH]
        there = pl.ds(c * REACH, REACH)
        return (
            Copy(own, YB.at[f - 1, there], (0, 1, 0)),
            Copy(own, YC.at[f - 1, there], (0, -1, 0)),
        )

    def send_z(f, low, high, dx=0):
        rows = pl.ds(H + low, high - low)
        there = pl.ds(H + low - dx * tx, high - low)
        return (
            Copy(F.at[f, rows, :, pl.ds(tz - LANES, LANES)], ZL.at[f - 1, there], (dx, 0, 1)),
            Copy(F.at[f, rows, :, pl.ds(0, LANES)], ZR.at[f - 1, there], (dx, 0, -1)),
        )

    groups = HALF // REACH

    def gather(rows, first):
        packed = None
        for k in range(REACH):
            row = rows[k]
            shift = (2 * k - first) % 8
            row = pltpu.roll(row, shift, 0) if shift else row
            packed = row if packed is None else jnp.where(sub_z // 2 == k, row, packed)
        return packed

    def pass_on(src, buf, s, g, dy):
        done = []
        if g < groups:
            done.append(Copy(src, buf.at[s, groups + nchunk + g], (-1, dy, 0)))
        if g >= nchunk - groups:
            done.append(Copy(src, buf.at[s, g - (nchunk - groups)], (1, dy, 0)))
        return done

    def send_rows(f, s, g):
        rows = [F[f, H + g * REACH + k] for k in range(REACH)]
        PS[s, 0, g] = gather(rows, 0)
        PS[s, 1, g] = gather(rows, 6)
        done = []
        for dy, side, buf in ((1, 1, YPB), (-1, 0, YPC)):
            src = PS.at[s, side, g]
            done.append(Copy(src, buf.at[s, groups + g], (0, dy, 0)))
            done += pass_on(src, buf, s, g, dy)
        return done

    def relay_rows(f, s, g):
        done = []
        for src, buf, first in ((YB, YPB, 6), (YC, YPC, 0)):
            buf[s, groups + g] = gather(
                [src[f - 1, g * REACH + k] for k in range(REACH)], first
            )
            done += pass_on(buf.at[s, groups + g], buf, s, g, 0)
        return done

    order = [0] + [nchunk - 1] * (nchunk > 1) + list(range(1, nchunk - 1))
    xw, yw, zw = {}, {}, {}
    xw[1] = send_x(1, 0, REACH)
    for c in order:
        yw[1, c] = send_y(1, c)
        zw[1, c] = send_z(1, c * REACH, (c + 1) * REACH)

    def zero(missing, *refs):
        @pl.when(missing)
        def _():
            for ref in refs:
                ref[...] = jnp.zeros(ref.shape, jnp.float32)

    low_rows, high_rows = pl.ds(0, H), pl.ds(H + tx, H)
    low_packs, high_packs = pl.ds(0, groups), pl.ds(groups + nchunk, groups)
    zero(low_x, *[F.at[i, low_rows] for i in range(1, STEPS + 2)])
    zero(high_x, *[F.at[i, high_rows] for i in range(1, STEPS + 2)])
    zero(low_y, YB, YPB)
    zero(high_y, YC, YPC)
    zero(low_z, ZL)
    zero(high_z, ZR)
    zero(low_x, *[b.at[snaps[s] - 1, low_rows] for b in (ZL, ZR) for s in range(nsnap)])
    zero(high_x, *[b.at[snaps[s] - 1, high_rows] for b in (ZL, ZR) for s in range(nsnap)])
    zero(low_x, *[b.at[s, low_packs] for b in (YPB, YPC) for s in range(nsnap)])
    zero(high_x, *[b.at[s, high_packs] for b in (YPB, YPC) for s in range(nsnap)])

    x_start, y_start, z_start = ix * tx, iy * ty, iz * tz

    def load_rest(x):
        F[0, H + x] = weave(1, x, sp[x], rp[x])
        damping = ab[x].astype(jnp.float32) / 16.0
        inverse = 1.0 / (1.0 + damping)
        c2 = cr[x] * inverse
        a2 = 2.0 * inverse + (3.0 * centre_weight) * c2
        b2 = (damping - 1.0) * inverse
        CA[x] = weave(2, x, a2, a2)
        CB[x] = weave(3, x, b2, b2)
        CC[x] = weave(4, x, c2, c2)
        rows = x * 8 + lax.broadcasted_iota(jnp.int32, (8, rc.shape[1]), 0)
        y_of = rc[1:2, :] - y_start
        where = (rc[0:1, :] - x_start) * 8 + y_of * 2 + 1
        where = jnp.where((y_of >= 0) & (y_of < ty), where, -1)
        top = jnp.where(iz == 0, 1.0, 0.0)
        for t in range(STEPS):
            total = jnp.sum(
                jnp.where(rows == where, tr[t : t + 1, :], 0.0), axis=1, keepdims=True
            )
            INJ[t, x] = jnp.where(lane == 0, total * top, 0.0)

    for c in fetched[2:]:
        c.wait()
    each(0, tx, load_rest, unroll=2)
    point = jnp.where(
        (lane_z == cell[2] - z_start) & (sub_z == (cell[1] - y_start) * 2), 1.0, 0.0
    )
    source_x = cell[0] - x_start

    def swap(v):
        parity = lax.broadcasted_iota(jnp.int32, v.shape, 0) % 2
        return jnp.where(parity == 0, pltpu.roll(v, 7, 0), pltpu.roll(v, 1, 0))

    def prepare(s, f):
        for w in late[s]:
            w.wait()

        def swapped(x):
            G[s, x] = swap(F[f, x])

        each(0, tx + 2 * H, swapped, unroll=5)

        def edges(x):
            edge = jnp.where(lane < LANES // 2, ZR[f - 1, x], ZL[f - 1, x])
            E[s, x] = edge
            GE[s, x] = swap(edge)

        each(H - HALF, H + tx + HALF, edges, unroll=4)

        def unpack(g):
            above, below = YPC[s, g], YPB[s, g]
            for j in range(REACH):
                first = pltpu.roll(above, (8 - 2 * j) % 8, 0) if j else above
                shift = (6 - 2 * j) % 8
                other = pltpu.roll(below, shift, 0) if shift else below
                both = jnp.where(sub_z < 4, first, other)
                D[s, g * REACH + j] = both
                DG[s, g * REACH + j] = swap(both)

        each(0, (tx + 2 * HALF) // REACH, unpack)

    def advance(t, c):
        f = t + 1

        def body(j):
            x = c * REACH + j
            cur = F[f, H + x]
            below, above = YB[t, x], YC[t, x]
            edge = jnp.where(lane < LANES // 2, ZR[t, H + x], ZL[t, H + x])
            row = jnp.concatenate([cur, edge], axis=1)
            wide = tz + LANES
            total = None
            for k, w in ((1, W1), (2, W2), (3, W3), (4, W4)):
                part = F[f, H + x + k] + F[f, H + x - k]
                part = part + (pltpu.roll(row, k, 1) + pltpu.roll(row, wide - k, 1))[:, :tz]
                if k == 4:
                    part = part + (above + below)
                total = w * part if total is None else total + w * part

            def up(k):
                return jnp.where(sub_z < 2 * k, above, cur)

            def down(k):
                return jnp.where(sub_z >= 8 - 2 * k, below, cur)

            total = total + pltpu.roll(W1 * up(1) + W3 * down(3), 6, 0)
            total = total + pltpu.roll(W2 * (up(2) + down(2)), 4, 0)
            total = total + pltpu.roll(W3 * up(3) + W1 * down(1), 2, 0)
            new = CA[x] * cur + CB[x] * F[f - 1, H + x] + CC[x] * total
            new = new + point * (wav[t] * (source_x == x).astype(jnp.float32))
            F[f + 1, H + x] = new
            F[f + 1, H + x, :, 0:LANES] = new[:, 0:LANES] + INJ[t, x]

        each(0, REACH, body, unroll=REACH)

    late = {}
    for t in range(STEPS):
        f = t + 1
        nf = f + 1
        last = t == STEPS - 1
        for number, c in enumerate(order):
            if number == 0:
                xw[f][1].wait()
                if nchunk == 1:
                    xw[f][0].wait()
            if number == 1:
                xw[f][0].wait()
            for w in yw[f, c] + zw[f, c]:
                w.wait()
            advance(t, c)
            if not last:
                yw[nf, c] = send_y(nf, c)
                zw[nf, c] = send_z(nf, c * REACH, (c + 1) * REACH)
                if number == min(1, nchunk - 1):
                    xw[nf] = send_x(nf, 0, REACH)
            elif nf in snaps:
                waits = late.setdefault(snaps.index(nf), [])
                waits += send_x_chunk(nf, c)
                waits += send_rows(nf, snaps.index(nf), c)
            if f in snaps:
                late[snaps.index(f)] += relay_rows(f, snaps.index(f), c)
        if nf in snaps:
            s = snaps.index(nf)
            waits = late.setdefault(s, [])
            if not last:
                waits += send_x(nf, REACH, H)
            else:
                waits += send_z(nf, 0, tx)
            waits += send_z(nf, 0, HALF, -1)
            waits += send_z(nf, tx - HALF, tx, 1)

    def out_fields(x):
        out_s[x], out_r[x] = unweave(x, F[STEPS + 1, H + x], (even, odd))

    each(0, tx, out_fields, unroll=4)
    leaving = [
        pltpu.make_async_copy(out_s, to_s, leave.at[LAGS]),
        pltpu.make_async_copy(out_r, to_r, leave.at[LAGS + 1]),
    ]
    for c in leaving:
        c.start()

    def lag_out(lag):
        return pltpu.make_async_copy(out_i.at[lag], to_i.at[lag], leave.at[lag])

    for s, f in enumerate(snaps):
        prepare(s, f)

    def image(m, keep_even, keep_odd):
        def product(x):
            a, b = HALF + x - m, HALF + x + m
            total = F[snaps[0], a] * G[0, b]
            for s in range(1, nsnap):
                total = total + F[snaps[s], a] * G[s, b]
            return total

        def halo(x):
            a, b = H + x - m, H + x + m
            edge = E[0, a] * GE[0, b]
            for s in range(1, nsnap):
                edge = edge + E[s, a] * GE[s, b]
            a, b = HALF + x - m, HALF + x + m
            side = D[0, a] * DG[0, b]
            for s in range(1, nsnap):
                side = side + D[s, a] * DG[s, b]
            return edge, side

        before, centre = product(0), product(1)
        for x in range(tx):
            after = product(x + 2)
            edge, side = halo(x)
            row = jnp.concatenate([centre, edge], axis=1)
            wide = tz + LANES
            near = (pltpu.roll(row, 1, 1) + pltpu.roll(row, wide - 1, 1))[:, :tz]
            near = near + (before + after)
            near = near + pltpu.roll(jnp.where(sub_z < 2, side, centre), 6, 0)
            near = near + pltpu.roll(jnp.where(sub_z >= 6, side, centre), 2, 0)
            plus, minus = unweave(x, 6.0 * centre - near, (even, odd))
            if keep_even:
                out_i[HALF + m, x] = plus.astype(jnp.bfloat16)
            if keep_odd:
                out_i[HALF - m, x] = minus.astype(jnp.bfloat16)
            before, centre = centre, after
        if keep_even:
            lag_out(HALF + m).start()
        if keep_odd:
            lag_out(HALF - m).start()

    image(0, True, False)
    each(1, HALF, lambda m: image(m, True, True))
    image(HALF, False, True)
    for c in copies:
        c.finish()
    for c in leaving:
        c.wait()
    each(0, LAGS, lambda lag: lag_out(lag).wait())


PARTS = 8


def deliver(s, r, i, out_s, out_r, out_i, held_s, held_r, held_i, arrive, leave):
    triples = [(s, held_s, out_s), (r, held_r, out_r)]
    part = LAGS // PARTS
    for k in range(PARTS):
        lags = pl.ds(k * part, part)
        triples.append((i.at[lags], held_i.at[lags], out_i.at[lags]))
    first = [pltpu.make_async_copy(a, b, arrive.at[n]) for n, (a, b, c) in enumerate(triples)]
    second = [pltpu.make_async_copy(b, c, leave.at[n]) for n, (a, b, c) in enumerate(triples)]
    for c in first:
        c.start()
    for one, two in zip(first, second):
        one.wait()
        two.start()
    for c in second:
        c.wait()


def local(
    source_prev,
    source_now,
    receiver_prev,
    receiver_now,
    courant,
    absorbing,
    source_cell,
    wavelet,
    receiver_cells,
    traces,
):
    tx, ty, tz = courant.shape
    nsnap = STEPS // EVERY
    nchunk = tx // REACH
    groups = (tx + 2 * HALF) // REACH
    f32 = jnp.float32
    number = STEPS * (2 + 4 * nchunk) + nsnap * 20
    V = pltpu.VMEM
    results = (
        jax.ShapeDtypeStruct((tx, ty, tz), f32),
        jax.ShapeDtypeStruct((tx, ty, tz), f32),
        jax.ShapeDtypeStruct((LAGS, tx, ty, tz), jnp.bfloat16),
    )
    far = pl.BlockSpec(memory_space=pltpu.HBM)
    moved = pl.pallas_call(
        kernel,
        out_shape=results,
        in_specs=[far] * 10,
        out_specs=(far, far, far),
        scratch_shapes=[
            V((tx, ty, tz), f32),
            V((tx, ty, tz), f32),
            V((LAGS, tx, ty, tz), jnp.bfloat16),
            V((STEPS + 2, tx + 2 * H, 8, tz), f32),
            V((STEPS, tx, 8, tz), f32),
            V((STEPS, tx, 8, tz), f32),
            V((STEPS + 1, tx + 2 * H, 8, LANES), f32),
            V((STEPS + 1, tx + 2 * H, 8, LANES), f32),
            V((nsnap, 2, nchunk, 8, tz), f32),
            V((nsnap, groups, 8, tz), f32),
            V((nsnap, groups, 8, tz), f32),
            V((nsnap, tx + 2 * H, 8, LANES), f32),
            V((nsnap, tx + 2 * H, 8, tz), f32),
            V((nsnap, tx + 2 * H, 8, LANES), f32),
            V((nsnap, tx + 2 * HALF, 8, tz), f32),
            V((nsnap, tx + 2 * HALF, 8, tz), f32),
            V((tx, 8, tz), f32),
            V((tx, 8, tz), f32),
            V((tx, 8, tz), f32),
            V((STEPS, tx, 8, LANES), f32),
            V((tx, tz // LANES, 8, LANES), f32),
            V((5, tx, tz // LANES, 8, LANES), f32),
            *[V((tx, ty, tz), f32) for _ in range(5)],
            V((tx, ty, tz), jnp.int32),
            pltpu.SMEM(source_cell.shape, jnp.int32),
            pltpu.SMEM(wavelet.shape, f32),
            V(receiver_cells.shape[::-1], jnp.int32),
            V(traces.shape, f32),
            pltpu.SemaphoreType.DMA((number,)),
            pltpu.SemaphoreType.DMA((number,)),
            pltpu.SemaphoreType.DMA((10,)),
            pltpu.SemaphoreType.DMA((LAGS + 2,)),
        ],
        compiler_params=pltpu.CompilerParams(
            collective_id=0, has_side_effects=True, vmem_limit_bytes=63 * 2**20
        ),
    )(
        source_prev,
        source_now,
        receiver_prev,
        receiver_now,
        courant,
        absorbing,
        source_cell,
        wavelet,
        receiver_cells.T,
        traces,
    )
    return pl.pallas_call(
        deliver,
        out_shape=results,
        in_specs=[far] * 3,
        out_specs=(far, far, far),
        scratch_shapes=[
            V((tx, ty, tz), f32),
            V((tx, ty, tz), f32),
            V((LAGS, tx, ty, tz), jnp.bfloat16),
            pltpu.SemaphoreType.DMA((PARTS + 2,)),
            pltpu.SemaphoreType.DMA((PARTS + 2,)),
        ],
        compiler_params=pltpu.CompilerParams(vmem_limit_bytes=63 * 2**20),
    )(*moved)


def solution(mesh):
    placed = (
        P(("shot", "gx"), "gy", "gz"),
        P(("shot", "gx"), "gy", "gz"),
        P(("shot", "gx"), "gy", "gz"),
        P(("shot", "gx"), "gy", "gz"),
        P("gx", "gy", "gz"),
        P("gx", "gy", "gz"),
        P("shot"),
        P("shot"),
        P("shot", None),
        P(None, "shot"),
    )
    return jax.shard_map(
        local,
        mesh=mesh,
        in_specs=placed,
        out_specs=(
            P(("shot", "gx"), "gy", "gz"),
            P(("shot", "gx"), "gy", "gz"),
            P(None, ("shot", "gx"), "gy", "gz"),
        ),
        check_vma=False,
    )
```

```python
import functools
import jax
import jax.numpy as jnp
from jax import lax
from jax.experimental import pallas as pl
from jax.experimental.pallas import tpu as pltpu
from jax.sharding import PartitionSpec as P

LAGS = 16
STEPS = 4
EVERY = 2
HALF = LAGS // 2
H = HALF + 1
REACH = 4
LANES = 128

W1, W2, W3, W4 = (8.0 / 5.0, -1.0 / 5.0, 8.0 / 315.0, -1.0 / 560.0)
centre_weight = -205.0 / 72.0
MESH = pl.DeviceIdType.MESH


def kernel(
    sp_in, sn_in, rp_in, rn_in, cr_in, ab_in, cell_in, wav_in, rc_in, tr_in,
    to_s, to_r, to_i,
    out_s, out_r, out_i,
    F, YB, YC, ZL, ZR, PS, YPB, YPC, E, G, GE, D, DG, CA, CB, CC, INJ, LP, ST,
    sp, sn, rp, rn, cr, ab, cell, wav, rc, tr,
    send, recv, fetch, leave,
):
    tx, ty, tz = sn.shape
    nchunk = tx // REACH
    snaps = [t + 2 for t in range(STEPS) if (t + 1) % EVERY == 0]
    nsnap = len(snaps)
    nx, ny, nz = (lax.axis_size(a) for a in ("gx", "gy", "gz"))
    ix, iy, iz = (lax.axis_index(a) for a in ("gx", "gy", "gz"))
    copies = []

    def exists(dx, dy, dz):
        ok = None
        for d, i, n in ((dx, ix, nx), (dy, iy, ny), (dz, iz, nz)):
            if d:
                here = (i + d >= 0) & (i + d < n)
                ok = here if ok is None else ok & here
        return ok

    def device(dx, dy, dz):
        return {
            a: i + d for a, i, d in (("gx", ix, dx), ("gy", iy, dy), ("gz", iz, dz)) if d
        }

    class Copy:
        def __init__(self, src, dst, direction):
            number = len(copies)
            self.desc = pltpu.make_async_remote_copy(
                src_ref=src,
                dst_ref=dst,
                send_sem=send.at[number],
                recv_sem=recv.at[number],
                device_id=device(*direction),
                device_id_type=MESH,
            )
            self.out = exists(*direction)
            self.into = exists(*(-d for d in direction))
            copies.append(self)
            pl.when(self.out)(lambda: self.desc.start())

        def wait(self):
            pl.when(self.into)(lambda: self.desc.wait_recv())

        def finish(self):
            pl.when(self.out)(lambda: self.desc.wait_send())

    lane = lax.broadcasted_iota(jnp.int32, (8, LANES), 1)
    sub_z = lax.broadcasted_iota(jnp.int32, (8, tz), 0)
    lane_z = lax.broadcasted_iota(jnp.int32, (8, tz), 1)
    even, odd = pl.ds(0, ty, 2), pl.ds(1, ty, 2)

    def each(low, high, body, unroll=1):
        def step(i, carry):
            body(i)
            return carry

        lax.fori_loop(low, high, step, 0, unroll=unroll)

    tiles = tz // LANES

    def weave(slot, x, a, b):
        for q in range(tiles):
            part = slice(q * LANES, (q + 1) * LANES)
            ST[slot, x, q, even, :] = a[:, part]
            ST[slot, x, q, odd, :] = b[:, part]
        return jnp.concatenate([ST[slot, x, q] for q in range(tiles)], axis=1)

    def unweave(x, v, at):
        for q in range(tiles):
            LP[x, q] = v[:, q * LANES : (q + 1) * LANES]
        return [
            jnp.concatenate([LP[x, q, rows, :] for q in range(tiles)], axis=1) for rows in at
        ]

    def load_now(x):
        F[1, H + x] = weave(0, x, sn[x], rn[x])

    low_x, high_x = ix == 0, ix == nx - 1
    low_y, high_y = iy == 0, iy == ny - 1
    low_z, high_z = iz == 0, iz == nz - 1

    signs = (-1, 1)
    around = [(s, 0, 0) for s in signs] + [(0, s, 0) for s in signs] + [(0, 0, s) for s in signs]
    around += [(s, r, 0) for s in signs for r in signs] + [(s, 0, r) for s in signs for r in signs]
    barrier = pltpu.get_barrier_semaphore()
    count = 0
    for direction in around:
        there = exists(*direction)
        count = count + there.astype(jnp.int32)

        @pl.when(there)
        def _(direction=direction):
            pl.semaphore_signal(
                barrier, inc=1, device_id=device(*direction), device_id_type=MESH
            )

    fetched = [
        pltpu.make_async_copy(src, dst, fetch.at[i])
        for i, (src, dst) in enumerate(
            (
                (sn_in, sn), (rn_in, rn), (sp_in, sp), (rp_in, rp), (cr_in, cr),
                (ab_in, ab), (cell_in, cell), (wav_in, wav), (rc_in, rc), (tr_in, tr),
            )
        )
    ]
    for c in fetched:
        c.start()
    for c in fetched[:2]:
        c.wait()
    each(0, tx, load_now, unroll=4)
    pl.semaphore_wait(barrier, count)

    def send_left(f, low, high):
        return Copy(
            F.at[f, H + low : H + high],
            F.at[f, H + tx + low : H + tx + high],
            (-1, 0, 0),
        )

    def send_right(f, low, high):
        return Copy(
            F.at[f, H + tx - high : H + tx - low],
            F.at[f, H - high : H - low],
            (1, 0, 0),
        )

    def send_x(f, low, high):
        return send_left(f, low, high), send_right(f, low, high)

    def send_x_chunk(f, c):
        done = []
        low, high = c * REACH, min((c + 1) * REACH, H)
        if low < high:
            done.append(
                Copy(F.at[f, H + low : H + high], F.at[f, H + tx + low : H + tx + high], (-1, 0, 0))
            )
        low, high = max(c * REACH, tx - H), (c + 1) * REACH
        if low < high:
            done.append(
                Copy(F.at[f, H + low : H + high], F.at[f, H + low - tx : H + high - tx], (1, 0, 0))
            )
        return done

    def send_y(f, c):
        own = F.at[f, H + c * REACH : H + (c + 1) * REACH]
        there = pl.ds(c * REACH, REACH)
        return (
            Copy(own, YB.at[f - 1, there], (0, 1, 0)),
            Copy(own, YC.at[f - 1, there], (0, -1, 0)),
        )

    def send_z(f, low, high, dx=0):
        rows = pl.ds(H + low, high - low)
        there = pl.ds(H + low - dx * tx, high - low)
        return (
            Copy(F.at[f, rows, :, pl.ds(tz - LANES, LANES)], ZL.at[f - 1, there], (dx, 0, 1)),
            Copy(F.at[f, rows, :, pl.ds(0, LANES)], ZR.at[f - 1, there], (dx, 0, -1)),
        )

    groups = HALF // REACH

    def gather(rows, first):
        packed = None
        for k in range(REACH):
            row = rows[k]
            shift = (2 * k - first) % 8
            row = pltpu.roll(row, shift, 0) if shift else row
            packed = row if packed is None else jnp.where(sub_z // 2 == k, row, packed)
        return packed

    def pass_on(src, buf, s, g, dy):
        done = []
        if g < groups:
            done.append(Copy(src, buf.at[s, groups + nchunk + g], (-1, dy, 0)))
        if g >= nchunk - groups:
            done.append(Copy(src, buf.at[s, g - (nchunk - groups)], (1, dy, 0)))
        return done

    def send_rows(f, s, g):
        rows = [F[f, H + g * REACH + k] for k in range(REACH)]
        PS[s, 0, g] = gather(rows, 0)
        PS[s, 1, g] = gather(rows, 6)
        done = []
        for dy, side, buf in ((1, 1, YPB), (-1, 0, YPC)):
            src = PS.at[s, side, g]
            done.append(Copy(src, buf.at[s, groups + g], (0, dy, 0)))
            done += pass_on(src, buf, s, g, dy)
        return done

    def relay_rows(f, s, g):
        done = []
        for src, buf, first in ((YB, YPB, 6), (YC, YPC, 0)):
            buf[s, groups + g] = gather(
                [src[f - 1, g * REACH + k] for k in range(REACH)], first
            )
            done += pass_on(buf.at[s, groups + g], buf, s, g, 0)
        return done

    order = [0] + [nchunk - 1] * (nchunk > 1) + list(range(1, nchunk - 1))
    xw, yw, zw = {}, {}, {}
    xw[1] = send_x(1, 0, REACH)
    for c in order:
        yw[1, c] = send_y(1, c)
        zw[1, c] = send_z(1, c * REACH, (c + 1) * REACH)

    def zero(missing, *refs):
        @pl.when(missing)
        def _():
            for ref in refs:
                ref[...] = jnp.zeros(ref.shape, jnp.float32)

    low_rows, high_rows = pl.ds(0, H), pl.ds(H + tx, H)
    low_packs, high_packs = pl.ds(0, groups), pl.ds(groups + nchunk, groups)
    zero(low_x, *[F.at[i, low_rows] for i in range(1, STEPS + 2)])
    zero(high_x, *[F.at[i, high_rows] for i in range(1, STEPS + 2)])
    zero(low_y, YB, YPB)
    zero(high_y, YC, YPC)
    zero(low_z, ZL)
    zero(high_z, ZR)
    zero(low_x, *[b.at[snaps[s] - 1, low_rows] for b in (ZL, ZR) for s in range(nsnap)])
    zero(high_x, *[b.at[snaps[s] - 1, high_rows] for b in (ZL, ZR) for s in range(nsnap)])
    zero(low_x, *[b.at[s, low_packs] for b in (YPB, YPC) for s in range(nsnap)])
    zero(high_x, *[b.at[s, high_packs] for b in (YPB, YPC) for s in range(nsnap)])

    x_start, y_start, z_start = ix * tx, iy * ty, iz * tz

    def load_rest(x):
        F[0, H + x] = weave(1, x, sp[x], rp[x])
        damping = ab[x].astype(jnp.float32) / 16.0
        inverse = 1.0 / (1.0 + damping)
        c2 = cr[x] * inverse
        a2 = 2.0 * inverse + (3.0 * centre_weight) * c2
        b2 = (damping - 1.0) * inverse
        CA[x] = weave(2, x, a2, a2)
        CB[x] = weave(3, x, b2, b2)
        CC[x] = weave(4, x, c2, c2)
        rows = x * 8 + lax.broadcasted_iota(jnp.int32, (8, rc.shape[1]), 0)
        y_of = rc[1:2, :] - y_start
        where = (rc[0:1, :] - x_start) * 8 + y_of * 2 + 1
        where = jnp.where((y_of >= 0) & (y_of < ty), where, -1)
        top = jnp.where(iz == 0, 1.0, 0.0)
        for t in range(STEPS):
            total = jnp.sum(
                jnp.where(rows == where, tr[t : t + 1, :], 0.0), axis=1, keepdims=True
            )
            INJ[t, x] = jnp.where(lane == 0, total * top, 0.0)

    for c in fetched[2:]:
        c.wait()
    each(0, tx, load_rest, unroll=2)
    point = jnp.where(
        (lane_z == cell[2] - z_start) & (sub_z == (cell[1] - y_start) * 2), 1.0, 0.0
    )
    source_x = cell[0] - x_start

    def swap(v):
        parity = lax.broadcasted_iota(jnp.int32, v.shape, 0) % 2
        return jnp.where(parity == 0, pltpu.roll(v, 7, 0), pltpu.roll(v, 1, 0))

    def prepare(s, f):
        def swapped(x):
            G[s, x] = swap(F[f, x])

        each(H, H + tx, swapped, unroll=6)
        for w in late[s]:
            w.wait()
        each(0, H, swapped, unroll=H)
        each(H + tx, 2 * H + tx, swapped, unroll=H)

        def edges(x):
            edge = jnp.where(lane < LANES // 2, ZR[f - 1, x], ZL[f - 1, x])
            E[s, x] = edge
            GE[s, x] = swap(edge)

        each(H - HALF, H + tx + HALF, edges, unroll=4)

        def unpack(g):
            above, below = YPC[s, g], YPB[s, g]
            for j in range(REACH):
                first = pltpu.roll(above, (8 - 2 * j) % 8, 0) if j else above
                shift = (6 - 2 * j) % 8
                other = pltpu.roll(below, shift, 0) if shift else below
                both = jnp.where(sub_z < 4, first, other)
                D[s, g * REACH + j] = both
                DG[s, g * REACH + j] = swap(both)

        each(0, (tx + 2 * HALF) // REACH, unpack)

    def advance(t, c):
        f = t + 1

        def body(j):
            x = c * REACH + j
            cur = F[f, H + x]
            below, above = YB[t, x], YC[t, x]
            edge = jnp.where(lane < LANES // 2, ZR[t, H + x], ZL[t, H + x])
            row = jnp.concatenate([cur, edge], axis=1)
            wide = tz + LANES
            total = None
            for k, w in ((1, W1), (2, W2), (3, W3), (4, W4)):
                part = F[f, H + x + k] + F[f, H + x - k]
                part = part + (pltpu.roll(row, k, 1) + pltpu.roll(row, wide - k, 1))[:, :tz]
                if k == 4:
                    part = part + (above + below)
                total = w * part if total is None else total + w * part

            def up(k):
                return jnp.where(sub_z < 2 * k, above, cur)

            def down(k):
                return jnp.where(sub_z >= 8 - 2 * k, below, cur)

            total = total + pltpu.roll(W1 * up(1) + W3 * down(3), 6, 0)
            total = total + pltpu.roll(W2 * (up(2) + down(2)), 4, 0)
            total = total + pltpu.roll(W3 * up(3) + W1 * down(1), 2, 0)
            new = CA[x] * cur + CB[x] * F[f - 1, H + x] + CC[x] * total
            new = new + point * (wav[t] * (source_x == x).astype(jnp.float32))
            F[f + 1, H + x] = new
            F[f + 1, H + x, :, 0:LANES] = new[:, 0:LANES] + INJ[t, x]

        each(0, REACH, body, unroll=REACH)

    late = {}
    for t in range(STEPS):
        f = t + 1
        nf = f + 1
        last = t == STEPS - 1
        for number, c in enumerate(order):
            if number == 0:
                xw[f][1].wait()
                if nchunk == 1:
                    xw[f][0].wait()
            if number == 1:
                xw[f][0].wait()
            for w in yw[f, c] + zw[f, c]:
                w.wait()
            advance(t, c)
            if not last:
                yw[nf, c] = send_y(nf, c)
                zw[nf, c] = send_z(nf, c * REACH, (c + 1) * REACH)
                if c == 0:
                    to_left = send_left(nf, 0, REACH)
                if c == nchunk - 1:
                    xw[nf] = to_left, send_right(nf, 0, REACH)
            elif nf in snaps:
                waits = late.setdefault(snaps.index(nf), [])
                waits += send_x_chunk(nf, c)
                waits += send_rows(nf, snaps.index(nf), c)
        if nf in snaps:
            s = snaps.index(nf)
            waits = late.setdefault(s, [])
            if not last:
                waits += send_x(nf, REACH, H)
            else:
                waits += send_z(nf, 0, tx)
            waits += send_z(nf, 0, HALF, -1)
            waits += send_z(nf, tx - HALF, tx, 1)
        if f in snaps:
            for g in range(nchunk):
                late[snaps.index(f)] += relay_rows(f, snaps.index(f), g)

    def out_fields(x):
        out_s[x], out_r[x] = unweave(x, F[STEPS + 1, H + x], (even, odd))

    each(0, tx, out_fields, unroll=4)
    leaving = [
        pltpu.make_async_copy(out_s, to_s, leave.at[LAGS]),
        pltpu.make_async_copy(out_r, to_r, leave.at[LAGS + 1]),
    ]
    for c in leaving:
        c.start()

    def lag_out(lag):
        return pltpu.make_async_copy(out_i.at[lag], to_i.at[lag], leave.at[lag])

    for s, f in enumerate(snaps):
        prepare(s, f)

    def image(m, keep_even, keep_odd):
        def product(x):
            a, b = HALF + x - m, HALF + x + m
            total = F[snaps[0], a] * G[0, b]
            for s in range(1, nsnap):
                total = total + F[snaps[s], a] * G[s, b]
            return total

        def halo(x):
            a, b = H + x - m, H + x + m
            edge = E[0, a] * GE[0, b]
            for s in range(1, nsnap):
                edge = edge + E[s, a] * GE[s, b]
            a, b = HALF + x - m, HALF + x + m
            side = D[0, a] * DG[0, b]
            for s in range(1, nsnap):
                side = side + D[s, a] * DG[s, b]
            return edge, side

        before, centre = product(0), product(1)
        for x in range(tx):
            after = product(x + 2)
            edge, side = halo(x)
            row = jnp.concatenate([centre, edge], axis=1)
            wide = tz + LANES
            near = (pltpu.roll(row, 1, 1) + pltpu.roll(row, wide - 1, 1))[:, :tz]
            near = near + (before + after)
            near = near + pltpu.roll(jnp.where(sub_z < 2, side, centre), 6, 0)
            near = near + pltpu.roll(jnp.where(sub_z >= 6, side, centre), 2, 0)
            plus, minus = unweave(x, 6.0 * centre - near, (even, odd))
            if keep_even:
                out_i[HALF + m, x] = plus.astype(jnp.bfloat16)
            if keep_odd:
                out_i[HALF - m, x] = minus.astype(jnp.bfloat16)
            before, centre = centre, after
        if keep_even:
            lag_out(HALF + m).start()
        if keep_odd:
            lag_out(HALF - m).start()

    image(0, True, False)
    each(1, HALF, lambda m: image(m, True, True))
    image(HALF, False, True)
    for c in copies:
        c.finish()
    for c in leaving:
        c.wait()
    each(0, LAGS, lambda lag: lag_out(lag).wait())


PARTS = 8


def deliver(s, r, i, out_s, out_r, out_i, held_s, held_r, held_i, arrive, leave):
    triples = [(s, held_s, out_s), (r, held_r, out_r)]
    part = LAGS // PARTS
    for k in range(PARTS):
        lags = pl.ds(k * part, part)
        triples.append((i.at[lags], held_i.at[lags], out_i.at[lags]))
    first = [pltpu.make_async_copy(a, b, arrive.at[n]) for n, (a, b, c) in enumerate(triples)]
    second = [pltpu.make_async_copy(b, c, leave.at[n]) for n, (a, b, c) in enumerate(triples)]
    for c in first:
        c.start()
    for one, two in zip(first, second):
        one.wait()
        two.start()
    for c in second:
        c.wait()


def local(
    source_prev,
    source_now,
    receiver_prev,
    receiver_now,
    courant,
    absorbing,
    source_cell,
    wavelet,
    receiver_cells,
    traces,
):
    tx, ty, tz = courant.shape
    nsnap = STEPS // EVERY
    nchunk = tx // REACH
    groups = (tx + 2 * HALF) // REACH
    f32 = jnp.float32
    number = STEPS * (2 + 4 * nchunk) + nsnap * 20
    V = pltpu.VMEM
    results = (
        jax.ShapeDtypeStruct((tx, ty, tz), f32),
        jax.ShapeDtypeStruct((tx, ty, tz), f32),
        jax.ShapeDtypeStruct((LAGS, tx, ty, tz), jnp.bfloat16),
    )
    far = pl.BlockSpec(memory_space=pltpu.HBM)
    moved = pl.pallas_call(
        kernel,
        out_shape=results,
        in_specs=[far] * 10,
        out_specs=(far, far, far),
        scratch_shapes=[
            V((tx, ty, tz), f32),
            V((tx, ty, tz), f32),
            V((LAGS, tx, ty, tz), jnp.bfloat16),
            V((STEPS + 2, tx + 2 * H, 8, tz), f32),
            V((STEPS, tx, 8, tz), f32),
            V((STEPS, tx, 8, tz), f32),
            V((STEPS + 1, tx + 2 * H, 8, LANES), f32),
            V((STEPS + 1, tx + 2 * H, 8, LANES), f32),
            V((nsnap, 2, nchunk, 8, tz), f32),
            V((nsnap, groups, 8, tz), f32),
            V((nsnap, groups, 8, tz), f32),
            V((nsnap, tx + 2 * H, 8, LANES), f32),
            V((nsnap, tx + 2 * H, 8, tz), f32),
            V((nsnap, tx + 2 * H, 8, LANES), f32),
            V((nsnap, tx + 2 * HALF, 8, tz), f32),
            V((nsnap, tx + 2 * HALF, 8, tz), f32),
            V((tx, 8, tz), f32),
            V((tx, 8, tz), f32),
            V((tx, 8, tz), f32),
            V((STEPS, tx, 8, LANES), f32),
            V((tx, tz // LANES, 8, LANES), f32),
            V((5, tx, tz // LANES, 8, LANES), f32),
            *[V((tx, ty, tz), f32) for _ in range(5)],
            V((tx, ty, tz), jnp.int32),
            pltpu.SMEM(source_cell.shape, jnp.int32),
            pltpu.SMEM(wavelet.shape, f32),
            V(receiver_cells.shape[::-1], jnp.int32),
            V(traces.shape, f32),
            pltpu.SemaphoreType.DMA((number,)),
            pltpu.SemaphoreType.DMA((number,)),
            pltpu.SemaphoreType.DMA((10,)),
            pltpu.SemaphoreType.DMA((LAGS + 2,)),
        ],
        compiler_params=pltpu.CompilerParams(
            collective_id=0, has_side_effects=True, vmem_limit_bytes=63 * 2**20
        ),
    )(
        source_prev,
        source_now,
        receiver_prev,
        receiver_now,
        courant,
        absorbing,
        source_cell,
        wavelet,
        receiver_cells.T,
        traces,
    )
    return pl.pallas_call(
        deliver,
        out_shape=results,
        in_specs=[far] * 3,
        out_specs=(far, far, far),
        scratch_shapes=[
            V((tx, ty, tz), f32),
            V((tx, ty, tz), f32),
            V((LAGS, tx, ty, tz), jnp.bfloat16),
            pltpu.SemaphoreType.DMA((PARTS + 2,)),
            pltpu.SemaphoreType.DMA((PARTS + 2,)),
        ],
        compiler_params=pltpu.CompilerParams(vmem_limit_bytes=63 * 2**20),
    )(*moved)


def solution(mesh):
    placed = (
        P(("shot", "gx"), "gy", "gz"),
        P(("shot", "gx"), "gy", "gz"),
        P(("shot", "gx"), "gy", "gz"),
        P(("shot", "gx"), "gy", "gz"),
        P("gx", "gy", "gz"),
        P("gx", "gy", "gz"),
        P("shot"),
        P("shot"),
        P("shot", None),
        P(None, "shot"),
    )
    return jax.shard_map(
        local,
        mesh=mesh,
        in_specs=placed,
        out_specs=(
            P(("shot", "gx"), "gy", "gz"),
            P(("shot", "gx"), "gy", "gz"),
            P(None, ("shot", "gx"), "gy", "gz"),
        ),
        check_vma=False,
    )
```

```python
import functools
import jax
import jax.numpy as jnp
from jax import lax
from jax.experimental import pallas as pl
from jax.experimental.pallas import tpu as pltpu
from jax.sharding import PartitionSpec as P

LAGS = 16
STEPS = 4
EVERY = 2
HALF = LAGS // 2
H = HALF + 1
REACH = 4
LANES = 128

W1, W2, W3, W4 = (8.0 / 5.0, -1.0 / 5.0, 8.0 / 315.0, -1.0 / 560.0)
centre_weight = -205.0 / 72.0
MESH = pl.DeviceIdType.MESH


def kernel(
    sp_in, sn_in, rp_in, rn_in, cr_in, ab_in, cell_in, wav_in, rc_in, tr_in,
    to_s, to_r, to_i,
    out_s, out_r, out_i,
    F, YB, YC, ZL, ZR, PS, YPB, YPC, E, G, GE, D, DG, CA, CB, CC, INJ, LP, ST,
    sp, sn, rp, rn, cr, ab, cell, wav, rc, tr,
    send, recv, fetch, leave,
):
    tx, ty, tz = sn.shape
    nchunk = tx // REACH
    snaps = [t + 2 for t in range(STEPS) if (t + 1) % EVERY == 0]
    nsnap = len(snaps)
    nx, ny, nz = (lax.axis_size(a) for a in ("gx", "gy", "gz"))
    ix, iy, iz = (lax.axis_index(a) for a in ("gx", "gy", "gz"))
    copies = []

    def exists(dx, dy, dz):
        ok = None
        for d, i, n in ((dx, ix, nx), (dy, iy, ny), (dz, iz, nz)):
            if d:
                here = (i + d >= 0) & (i + d < n)
                ok = here if ok is None else ok & here
        return ok

    def device(dx, dy, dz):
        return {
            a: i + d for a, i, d in (("gx", ix, dx), ("gy", iy, dy), ("gz", iz, dz)) if d
        }

    class Copy:
        def __init__(self, src, dst, direction):
            number = len(copies)
            self.desc = pltpu.make_async_remote_copy(
                src_ref=src,
                dst_ref=dst,
                send_sem=send.at[number],
                recv_sem=recv.at[number],
                device_id=device(*direction),
                device_id_type=MESH,
            )
            self.out = exists(*direction)
            self.into = exists(*(-d for d in direction))
            copies.append(self)
            pl.when(self.out)(lambda: self.desc.start())

        def wait(self):
            pl.when(self.into)(lambda: self.desc.wait_recv())

        def finish(self):
            pl.when(self.out)(lambda: self.desc.wait_send())

    lane = lax.broadcasted_iota(jnp.int32, (8, LANES), 1)
    sub_z = lax.broadcasted_iota(jnp.int32, (8, tz), 0)
    lane_z = lax.broadcasted_iota(jnp.int32, (8, tz), 1)
    even, odd = pl.ds(0, ty, 2), pl.ds(1, ty, 2)

    def each(low, high, body, unroll=1):
        def step(i, carry):
            body(i)
            return carry

        lax.fori_loop(low, high, step, 0, unroll=unroll)

    tiles = tz // LANES

    def weave(slot, x, a, b):
        for q in range(tiles):
            part = slice(q * LANES, (q + 1) * LANES)
            ST[slot, x, q, even, :] = a[:, part]
            ST[slot, x, q, odd, :] = b[:, part]
        return jnp.concatenate([ST[slot, x, q] for q in range(tiles)], axis=1)

    def unweave(x, v, at):
        for q in range(tiles):
            LP[x, q] = v[:, q * LANES : (q + 1) * LANES]
        return [
            jnp.concatenate([LP[x, q, rows, :] for q in range(tiles)], axis=1) for rows in at
        ]

    def load_now(x):
        F[1, H + x] = weave(0, x, sn[x], rn[x])

    low_x, high_x = ix == 0, ix == nx - 1
    low_y, high_y = iy == 0, iy == ny - 1
    low_z, high_z = iz == 0, iz == nz - 1

    signs = (-1, 1)
    around = [(s, 0, 0) for s in signs] + [(0, s, 0) for s in signs] + [(0, 0, s) for s in signs]
    around += [(s, r, 0) for s in signs for r in signs] + [(s, 0, r) for s in signs for r in signs]
    barrier = pltpu.get_barrier_semaphore()
    count = 0
    for direction in around:
        there = exists(*direction)
        count = count + there.astype(jnp.int32)

        @pl.when(there)
        def _(direction=direction):
            pl.semaphore_signal(
                barrier, inc=1, device_id=device(*direction), device_id_type=MESH
            )

    fetched = [
        pltpu.make_async_copy(src, dst, fetch.at[i])
        for i, (src, dst) in enumerate(
            (
                (sn_in, sn), (rn_in, rn), (sp_in, sp), (rp_in, rp), (cr_in, cr),
                (ab_in, ab), (cell_in, cell), (wav_in, wav), (rc_in, rc), (tr_in, tr),
            )
        )
    ]
    for c in fetched:
        c.start()
    for c in fetched[:2]:
        c.wait()
    each(0, REACH, load_now, unroll=REACH)
    pl.semaphore_wait(barrier, count)

    def send_left(f, low, high):
        return Copy(
            F.at[f, H + low : H + high],
            F.at[f, H + tx + low : H + tx + high],
            (-1, 0, 0),
        )

    def send_right(f, low, high):
        return Copy(
            F.at[f, H + tx - high : H + tx - low],
            F.at[f, H - high : H - low],
            (1, 0, 0),
        )

    def send_x(f, low, high):
        return send_left(f, low, high), send_right(f, low, high)

    def send_x_chunk(f, c):
        done = []
        low, high = c * REACH, min((c + 1) * REACH, H)
        if low < high:
            done.append(
                Copy(F.at[f, H + low : H + high], F.at[f, H + tx + low : H + tx + high], (-1, 0, 0))
            )
        low, high = max(c * REACH, tx - H), (c + 1) * REACH
        if low < high:
            done.append(
                Copy(F.at[f, H + low : H + high], F.at[f, H + low - tx : H + high - tx], (1, 0, 0))
            )
        return done

    def send_y(f, c):
        own = F.at[f, H + c * REACH : H + (c + 1) * REACH]
        there = pl.ds(c * REACH, REACH)
        return (
            Copy(own, YB.at[f - 1, there], (0, 1, 0)),
            Copy(own, YC.at[f - 1, there], (0, -1, 0)),
        )

    def send_z(f, low, high, dx=0):
        rows = pl.ds(H + low, high - low)
        there = pl.ds(H + low - dx * tx, high - low)
        return (
            Copy(F.at[f, rows, :, pl.ds(tz - LANES, LANES)], ZL.at[f - 1, there], (dx, 0, 1)),
            Copy(F.at[f, rows, :, pl.ds(0, LANES)], ZR.at[f - 1, there], (dx, 0, -1)),
        )

    groups = HALF // REACH

    def gather(rows, first):
        packed = None
        for k in range(REACH):
            row = rows[k]
            shift = (2 * k - first) % 8
            row = pltpu.roll(row, shift, 0) if shift else row
            packed = row if packed is None else jnp.where(sub_z // 2 == k, row, packed)
        return packed

    def pass_on(src, buf, s, g, dy):
        done = []
        if g < groups:
            done.append(Copy(src, buf.at[s, groups + nchunk + g], (-1, dy, 0)))
        if g >= nchunk - groups:
            done.append(Copy(src, buf.at[s, g - (nchunk - groups)], (1, dy, 0)))
        return done

    def send_rows(f, s, g):
        rows = [F[f, H + g * REACH + k] for k in range(REACH)]
        PS[s, 0, g] = gather(rows, 0)
        PS[s, 1, g] = gather(rows, 6)
        done = []
        for dy, side, buf in ((1, 1, YPB), (-1, 0, YPC)):
            src = PS.at[s, side, g]
            done.append(Copy(src, buf.at[s, groups + g], (0, dy, 0)))
            done += pass_on(src, buf, s, g, dy)
        return done

    def relay_rows(f, s, g):
        done = []
        for src, buf, first in ((YB, YPB, 6), (YC, YPC, 0)):
            buf[s, groups + g] = gather(
                [src[f - 1, g * REACH + k] for k in range(REACH)], first
            )
            done += pass_on(buf.at[s, groups + g], buf, s, g, 0)
        return done

    order = [0] + [nchunk - 1] * (nchunk > 1) + list(range(1, nchunk - 1))
    xw, yw, zw = {}, {}, {}
    for c in order:
        if c:
            each(c * REACH, (c + 1) * REACH, load_now, unroll=REACH)
        yw[1, c] = send_y(1, c)
        zw[1, c] = send_z(1, c * REACH, (c + 1) * REACH)
        if c == 0:
            to_left = send_left(1, 0, REACH)
        if c == nchunk - 1:
            xw[1] = to_left, send_right(1, 0, REACH)

    def zero(missing, *refs):
        @pl.when(missing)
        def _():
            for ref in refs:
                ref[...] = jnp.zeros(ref.shape, jnp.float32)

    low_rows, high_rows = pl.ds(0, H), pl.ds(H + tx, H)
    low_packs, high_packs = pl.ds(0, groups), pl.ds(groups + nchunk, groups)
    zero(low_x, *[F.at[i, low_rows] for i in range(1, STEPS + 2)])
    zero(high_x, *[F.at[i, high_rows] for i in range(1, STEPS + 2)])
    zero(low_y, YB, YPB)
    zero(high_y, YC, YPC)
    zero(low_z, ZL)
    zero(high_z, ZR)
    zero(low_x, *[b.at[snaps[s] - 1, low_rows] for b in (ZL, ZR) for s in range(nsnap)])
    zero(high_x, *[b.at[snaps[s] - 1, high_rows] for b in (ZL, ZR) for s in range(nsnap)])
    zero(low_x, *[b.at[s, low_packs] for b in (YPB, YPC) for s in range(nsnap)])
    zero(high_x, *[b.at[s, high_packs] for b in (YPB, YPC) for s in range(nsnap)])

    x_start, y_start, z_start = ix * tx, iy * ty, iz * tz

    def load_rest(x):
        F[0, H + x] = weave(1, x, sp[x], rp[x])
        damping = ab[x].astype(jnp.float32) / 16.0
        inverse = 1.0 / (1.0 + damping)
        c2 = cr[x] * inverse
        a2 = 2.0 * inverse + (3.0 * centre_weight) * c2
        b2 = (damping - 1.0) * inverse
        CA[x] = weave(2, x, a2, a2)
        CB[x] = weave(3, x, b2, b2)
        CC[x] = weave(4, x, c2, c2)
        rows = x * 8 + lax.broadcasted_iota(jnp.int32, (8, rc.shape[1]), 0)
        y_of = rc[1:2, :] - y_start
        where = (rc[0:1, :] - x_start) * 8 + y_of * 2 + 1
        where = jnp.where((y_of >= 0) & (y_of < ty), where, -1)
        top = jnp.where(iz == 0, 1.0, 0.0)
        for t in range(STEPS):
            total = jnp.sum(
                jnp.where(rows == where, tr[t : t + 1, :], 0.0), axis=1, keepdims=True
            )
            INJ[t, x] = jnp.where(lane == 0, total * top, 0.0)

    for c in fetched[2:]:
        c.wait()
    each(0, tx, load_rest, unroll=2)
    point = jnp.where(
        (lane_z == cell[2] - z_start) & (sub_z == (cell[1] - y_start) * 2), 1.0, 0.0
    )
    source_x = cell[0] - x_start

    def swap(v):
        parity = lax.broadcasted_iota(jnp.int32, v.shape, 0) % 2
        return jnp.where(parity == 0, pltpu.roll(v, 7, 0), pltpu.roll(v, 1, 0))

    def prepare(s, f):
        def swapped(x):
            G[s, x] = swap(F[f, x])

        each(H, H + tx, swapped, unroll=6)
        for w in late[s]:
            w.wait()
        each(0, H, swapped, unroll=H)
        each(H + tx, 2 * H + tx, swapped, unroll=H)

        def edges(x):
            edge = jnp.where(lane < LANES // 2, ZR[f - 1, x], ZL[f - 1, x])
            E[s, x] = edge
            GE[s, x] = swap(edge)

        each(H - HALF, H + tx + HALF, edges, unroll=4)

        def unpack(g):
            above, below = YPC[s, g], YPB[s, g]
            for j in range(REACH):
                first = pltpu.roll(above, (8 - 2 * j) % 8, 0) if j else above
                shift = (6 - 2 * j) % 8
                other = pltpu.roll(below, shift, 0) if shift else below
                both = jnp.where(sub_z < 4, first, other)
                D[s, g * REACH + j] = both
                DG[s, g * REACH + j] = swap(both)

        each(0, (tx + 2 * HALF) // REACH, unpack)

    def advance(t, c):
        f = t + 1

        def body(j):
            x = c * REACH + j
            cur = F[f, H + x]
            below, above = YB[t, x], YC[t, x]
            edge = jnp.where(lane < LANES // 2, ZR[t, H + x], ZL[t, H + x])
            row = jnp.concatenate([cur, edge], axis=1)
            wide = tz + LANES
            total = None
            for k, w in ((1, W1), (2, W2), (3, W3), (4, W4)):
                part = F[f, H + x + k] + F[f, H + x - k]
                part = part + (pltpu.roll(row, k, 1) + pltpu.roll(row, wide - k, 1))[:, :tz]
                if k == 4:
                    part = part + (above + below)
                total = w * part if total is None else total + w * part

            def up(k):
                return jnp.where(sub_z < 2 * k, above, cur)

            def down(k):
                return jnp.where(sub_z >= 8 - 2 * k, below, cur)

            total = total + pltpu.roll(W1 * up(1) + W3 * down(3), 6, 0)
            total = total + pltpu.roll(W2 * (up(2) + down(2)), 4, 0)
            total = total + pltpu.roll(W3 * up(3) + W1 * down(1), 2, 0)
            new = CA[x] * cur + CB[x] * F[f - 1, H + x] + CC[x] * total
            new = new + point * (wav[t] * (source_x == x).astype(jnp.float32))
            F[f + 1, H + x] = new
            F[f + 1, H + x, :, 0:LANES] = new[:, 0:LANES] + INJ[t, x]

        each(0, REACH, body, unroll=REACH)

    late = {}
    for t in range(STEPS):
        f = t + 1
        nf = f + 1
        last = t == STEPS - 1
        for number, c in enumerate(order):
            if number == 0:
                xw[f][1].wait()
                if nchunk == 1:
                    xw[f][0].wait()
            if number == 1:
                xw[f][0].wait()
            for w in yw[f, c] + zw[f, c]:
                w.wait()
            advance(t, c)
            if not last:
                yw[nf, c] = send_y(nf, c)
                zw[nf, c] = send_z(nf, c * REACH, (c + 1) * REACH)
                if c == 0:
                    to_left = send_left(nf, 0, REACH)
                if c == nchunk - 1:
                    xw[nf] = to_left, send_right(nf, 0, REACH)
            elif nf in snaps:
                waits = late.setdefault(snaps.index(nf), [])
                waits += send_x_chunk(nf, c)
                waits += send_rows(nf, snaps.index(nf), c)
        if nf in snaps:
            s = snaps.index(nf)
            waits = late.setdefault(s, [])
            if not last:
                waits += send_x(nf, REACH, H)
            else:
                waits += send_z(nf, 0, tx)
            waits += send_z(nf, 0, HALF, -1)
            waits += send_z(nf, tx - HALF, tx, 1)
        if f in snaps:
            for g in range(nchunk):
                late[snaps.index(f)] += relay_rows(f, snaps.index(f), g)

    def out_fields(x):
        out_s[x], out_r[x] = unweave(x, F[STEPS + 1, H + x], (even, odd))

    each(0, tx, out_fields, unroll=4)
    leaving = [
        pltpu.make_async_copy(out_s, to_s, leave.at[LAGS]),
        pltpu.make_async_copy(out_r, to_r, leave.at[LAGS + 1]),
    ]
    for c in leaving:
        c.start()

    def lag_out(lag):
        return pltpu.make_async_copy(out_i.at[lag], to_i.at[lag], leave.at[lag])

    for s, f in enumerate(snaps):
        prepare(s, f)

    def image(m, keep_even, keep_odd):
        def product(x):
            a, b = HALF + x - m, HALF + x + m
            total = F[snaps[0], a] * G[0, b]
            for s in range(1, nsnap):
                total = total + F[snaps[s], a] * G[s, b]
            return total

        def halo(x):
            a, b = H + x - m, H + x + m
            edge = E[0, a] * GE[0, b]
            for s in range(1, nsnap):
                edge = edge + E[s, a] * GE[s, b]
            a, b = HALF + x - m, HALF + x + m
            side = D[0, a] * DG[0, b]
            for s in range(1, nsnap):
                side = side + D[s, a] * DG[s, b]
            return edge, side

        before, centre = product(0), product(1)
        for x in range(tx):
            after = product(x + 2)
            edge, side = halo(x)
            row = jnp.concatenate([centre, edge], axis=1)
            wide = tz + LANES
            near = (pltpu.roll(row, 1, 1) + pltpu.roll(row, wide - 1, 1))[:, :tz]
            near = near + (before + after)
            near = near + pltpu.roll(jnp.where(sub_z < 2, side, centre), 6, 0)
            near = near + pltpu.roll(jnp.where(sub_z >= 6, side, centre), 2, 0)
            plus, minus = unweave(x, 6.0 * centre - near, (even, odd))
            if keep_even:
                out_i[HALF + m, x] = plus.astype(jnp.bfloat16)
            if keep_odd:
                out_i[HALF - m, x] = minus.astype(jnp.bfloat16)
            before, centre = centre, after
        if keep_even:
            lag_out(HALF + m).start()
        if keep_odd:
            lag_out(HALF - m).start()

    image(0, True, False)
    each(1, HALF, lambda m: image(m, True, True))
    image(HALF, False, True)
    for c in copies:
        c.finish()
    for c in leaving:
        c.wait()
    each(0, LAGS, lambda lag: lag_out(lag).wait())


PARTS = 8


def deliver(s, r, i, out_s, out_r, out_i, held_s, held_r, held_i, arrive, leave):
    triples = [(s, held_s, out_s), (r, held_r, out_r)]
    part = LAGS // PARTS
    for k in range(PARTS):
        lags = pl.ds(k * part, part)
        triples.append((i.at[lags], held_i.at[lags], out_i.at[lags]))
    first = [pltpu.make_async_copy(a, b, arrive.at[n]) for n, (a, b, c) in enumerate(triples)]
    second = [pltpu.make_async_copy(b, c, leave.at[n]) for n, (a, b, c) in enumerate(triples)]
    for c in first:
        c.start()
    for one, two in zip(first, second):
        one.wait()
        two.start()
    for c in second:
        c.wait()


def local(
    source_prev,
    source_now,
    receiver_prev,
    receiver_now,
    courant,
    absorbing,
    source_cell,
    wavelet,
    receiver_cells,
    traces,
):
    tx, ty, tz = courant.shape
    nsnap = STEPS // EVERY
    nchunk = tx // REACH
    groups = (tx + 2 * HALF) // REACH
    f32 = jnp.float32
    number = STEPS * (2 + 4 * nchunk) + nsnap * 20
    V = pltpu.VMEM
    results = (
        jax.ShapeDtypeStruct((tx, ty, tz), f32),
        jax.ShapeDtypeStruct((tx, ty, tz), f32),
        jax.ShapeDtypeStruct((LAGS, tx, ty, tz), jnp.bfloat16),
    )
    far = pl.BlockSpec(memory_space=pltpu.HBM)
    moved = pl.pallas_call(
        kernel,
        out_shape=results,
        in_specs=[far] * 10,
        out_specs=(far, far, far),
        scratch_shapes=[
            V((tx, ty, tz), f32),
            V((tx, ty, tz), f32),
            V((LAGS, tx, ty, tz), jnp.bfloat16),
            V((STEPS + 2, tx + 2 * H, 8, tz), f32),
            V((STEPS, tx, 8, tz), f32),
            V((STEPS, tx, 8, tz), f32),
            V((STEPS + 1, tx + 2 * H, 8, LANES), f32),
            V((STEPS + 1, tx + 2 * H, 8, LANES), f32),
            V((nsnap, 2, nchunk, 8, tz), f32),
            V((nsnap, groups, 8, tz), f32),
            V((nsnap, groups, 8, tz), f32),
            V((nsnap, tx + 2 * H, 8, LANES), f32),
            V((nsnap, tx + 2 * H, 8, tz), f32),
            V((nsnap, tx + 2 * H, 8, LANES), f32),
            V((nsnap, tx + 2 * HALF, 8, tz), f32),
            V((nsnap, tx + 2 * HALF, 8, tz), f32),
            V((tx, 8, tz), f32),
            V((tx, 8, tz), f32),
            V((tx, 8, tz), f32),
            V((STEPS, tx, 8, LANES), f32),
            V((tx, tz // LANES, 8, LANES), f32),
            V((5, tx, tz // LANES, 8, LANES), f32),
            *[V((tx, ty, tz), f32) for _ in range(5)],
            V((tx, ty, tz), jnp.int32),
            pltpu.SMEM(source_cell.shape, jnp.int32),
            pltpu.SMEM(wavelet.shape, f32),
            V(receiver_cells.shape[::-1], jnp.int32),
            V(traces.shape, f32),
            pltpu.SemaphoreType.DMA((number,)),
            pltpu.SemaphoreType.DMA((number,)),
            pltpu.SemaphoreType.DMA((10,)),
            pltpu.SemaphoreType.DMA((LAGS + 2,)),
        ],
        compiler_params=pltpu.CompilerParams(
            collective_id=0, has_side_effects=True, vmem_limit_bytes=63 * 2**20
        ),
    )(
        source_prev,
        source_now,
        receiver_prev,
        receiver_now,
        courant,
        absorbing,
        source_cell,
        wavelet,
        receiver_cells.T,
        traces,
    )
    return pl.pallas_call(
        deliver,
        out_shape=results,
        in_specs=[far] * 3,
        out_specs=(far, far, far),
        scratch_shapes=[
            V((tx, ty, tz), f32),
            V((tx, ty, tz), f32),
            V((LAGS, tx, ty, tz), jnp.bfloat16),
            pltpu.SemaphoreType.DMA((PARTS + 2,)),
            pltpu.SemaphoreType.DMA((PARTS + 2,)),
        ],
        compiler_params=pltpu.CompilerParams(vmem_limit_bytes=63 * 2**20),
    )(*moved)


def solution(mesh):
    placed = (
        P(("shot", "gx"), "gy", "gz"),
        P(("shot", "gx"), "gy", "gz"),
        P(("shot", "gx"), "gy", "gz"),
        P(("shot", "gx"), "gy", "gz"),
        P("gx", "gy", "gz"),
        P("gx", "gy", "gz"),
        P("shot"),
        P("shot"),
        P("shot", None),
        P(None, "shot"),
    )
    return jax.shard_map(
        local,
        mesh=mesh,
        in_specs=placed,
        out_specs=(
            P(("shot", "gx"), "gy", "gz"),
            P(("shot", "gx"), "gy", "gz"),
            P(None, ("shot", "gx"), "gy", "gz"),
        ),
        check_vma=False,
    )
```
